32 devices in a mesh: shard: 8 (over y, x, core), tensor: 4 (over z).
Axes of the slice: x: 2, y: 2, z: 4, core: 2. Of those that a mesh axis runs over, the one named last changes fastest.
Arguments:
- grads: bfloat16 [32, 1024, 1024], P(None, 'shard', 'tensor'), may hold values from -48 to 48
- momentum: float32 [32, 1024, 1024], P(None, 'shard', 'tensor'), may hold values from -6 to 6
Outputs:
- momentum_next: float32 [32, 1024, 1024], P(None, 'shard', 'tensor')
- update: bfloat16 [32, 1024, 1024], P(None, 'shard', 'tensor')
The draws below stay inside these ranges and needn't reach their ends.
All inputs are finite; a program needn't handle non-finite values.
Results may differ from the reference program's by a relative error of at most 0.012.
Values may be sent and summed in bfloat16 or wider, within the bound.
No kernel may reach another device: no remote copies, remote signals or barrier semaphores. Data moves between devices by JAX's collectives and lax.ppermute only.
A program may use at most 64 MiB of HBM per device.

```python
import jax
import jax.numpy as jnp
from jax import lax

D = 1024
NS_STEPS = 2
MATS = 32


def draw_grads(key, part):
    key_base, key_rows, key_cols = jax.random.split(jax.random.fold_in(key, 17), 3)
    rows = jnp.exp(jax.random.uniform(key_rows, (MATS, D, 1), jnp.float32) * 2.302585) / 3.1622777
    cols = jnp.exp(jax.random.uniform(key_cols, (MATS, 1, D), jnp.float32) * 2.302585) / 3.1622777
    base = jnp.clip(jax.random.normal(key_base, (MATS, D, D), jnp.float32), -4.0, 4.0)
    return (base * rows * cols).astype(jnp.bfloat16)


def steps_of(own_key, extent, cuts, smallest, top_value):
    factor_of, own = 1.0, jax.random.fold_in(own_key, 6)
    for dim, blocks in cuts:
        draws = jnp.exp(jax.random.uniform(jax.random.fold_in(own, dim), (blocks,), jnp.float32, smallest / len(cuts), top_value / len(cuts)))
        factor_of = factor_of * jnp.repeat(draws, extent[dim] // blocks).reshape([-1 if axis == dim else 1 for axis in range(len(extent))])
    return factor_of


def bell_draw(own_key, shape, deviation, most, cuts=(), dtype=jnp.bfloat16):
    entries = jax.random.normal(own_key, shape, jnp.float32) * deviation
    if len(cuts) > 0:
        entries = steps_of(own_key, shape, cuts, -0.22, 0.18) * entries
    return jnp.clip(entries, min=-most, max=most).astype(dtype)


def setup_inputs(seed: int = 0) -> dict:
    splits = jax.random.split(jax.random.key(seed), 3)
    return {
        "grads": draw_grads(jax.random.fold_in(splits[2], 71), 0),
        "momentum": bell_draw(splits[1], (MATS, D, D), 1.0, 6.0, ((1, 8), (2, 4)), jnp.float32),
    }


def dot32(left, right):
    return jnp.dot(left.astype(jnp.float32), right.astype(jnp.float32), precision=lax.Precision.HIGHEST)

def orthogonalize(nesterov):
    values = nesterov.astype(jnp.float32)
    norm_value = jnp.sqrt(jnp.sum(values * values))
    current = (values / (norm_value + 1e-07)).astype(jnp.bfloat16)
    for step in range(NS_STEPS):
        gram = dot32(current, current.T).astype(jnp.bfloat16)
        power_f = dot32(gram, current)
        power = power_f.astype(jnp.bfloat16)
        square = dot32(gram, power)
        current = (3.4445 * current.astype(jnp.float32) - 4.775 * power_f + 2.0315 * square).astype(jnp.bfloat16)
    scale = 0.2 * float(D) ** 0.5
    return (scale * current.astype(jnp.float32)).astype(jnp.bfloat16)

def reference(grads, momentum):
    momentum_next = 0.95 * momentum + grads.astype(jnp.float32)
    nesterov = (grads.astype(jnp.float32) + 0.95 * momentum_next).astype(jnp.bfloat16)
    update = lax.map(orthogonalize, nesterov)
    return (momentum_next, update)
```

```python
import jax
import jax.numpy as jnp
from jax import lax
from jax.sharding import PartitionSpec as P

NS_STEPS = 2


def dot_rows(left, right):
    return lax.dot_general(left, right, (((1,), (1,)), ((), ())), preferred_element_type=jnp.float32)


def dot(left, right):
    return jnp.dot(left, right, preferred_element_type=jnp.float32)


def chain(first, *rest):
    return lax.optimization_barrier((first,) + rest)


def swap(piece, count, k):
    return lax.ppermute(piece, "tensor", [(t, t ^ k) for t in range(count)])


def spread(piece):
    return lax.all_to_all(piece, "shard", split_axis=0, concat_axis=0, tiled=True)


def exchange(pieces, count):
    half = count // 2
    out = {}
    early = swap(pieces[half], count, half)
    late = [k for k in range(half + 1, count)]
    for k in reversed(late):
        out[k] = swap(spread(pieces[k]), count, k)
    rest = [k for k in range(half)]
    both = jnp.concatenate([pieces[k] for k in rest], axis=1)
    both = spread(both)
    rows = pieces[0].shape[1]
    for i, k in enumerate(rest):
        part = both[:, i * rows : (i + 1) * rows]
        out[k] = part if k == 0 else swap(part, count, k)
    out[half] = spread(early)
    return out


def shards(grads, momentum):
    grads_f = grads.astype(jnp.float32)
    momentum_next = 0.95 * momentum + grads_f
    shard_count = lax.axis_size("shard")
    tensor_count = lax.axis_size("tensor")
    count, row_part, col_part = grads.shape
    me = lax.axis_index("tensor")

    def nesterov(k):
        start = (me ^ k) * shard_count
        g = lax.dynamic_slice_in_dim(grads, start, shard_count, 0).astype(jnp.float32)
        m = lax.dynamic_slice_in_dim(momentum, start, shard_count, 0)
        return (g + 0.95 * (0.95 * m + g)).astype(jnp.bfloat16)

    pieces = {k: nesterov(k) for k in range(tensor_count)}
    got = exchange(pieces, tensor_count)
    order = shard_count * row_part
    xs = {k: got[k].reshape(order, col_part) for k in got}

    total = sum(jnp.sum(jnp.square(x.astype(jnp.float32))) for x in xs.values())
    scale = 1.0 / (jnp.sqrt(total) + 1e-07)
    for step in range(NS_STEPS):
        gram = sum(dot_rows(x, x) for x in xs.values())
        if step == 0:
            gram = gram * (scale * scale)
        gram = gram.astype(jnp.bfloat16)
        new = {}
        for k, x in xs.items():
            power_f = dot(gram, x)
            current = x.astype(jnp.float32)
            if step == 0:
                power_f = power_f * scale
                current = current * scale
            square = dot(gram, power_f.astype(jnp.bfloat16))
            new[k] = (3.4445 * current - 4.775 * power_f + 2.0315 * square).astype(jnp.bfloat16)
        xs = new
    gain = 0.2 * float(order) ** 0.5
    back = {
        k: (gain * x.astype(jnp.float32)).astype(jnp.bfloat16).reshape(shard_count, row_part, col_part)
        for k, x in xs.items()
    }
    done = exchange(back, tensor_count)
    update = jnp.zeros(grads.shape, jnp.bfloat16)
    for k in range(tensor_count):
        update = lax.dynamic_update_slice_in_dim(update, done[k], (me ^ k) * shard_count, 0)
    return (momentum_next, update)


def solution(mesh):
    return jax.shard_map(
        shards,
        mesh=mesh,
        in_specs=(P(None, "shard", "tensor"), P(None, "shard", "tensor")),
        out_specs=(P(None, "shard", "tensor"), P(None, "shard", "tensor")),
        check_vma=False,
    )
```

```python
import functools

import jax
import jax.numpy as jnp
from jax import lax
from jax.experimental import pallas as pl
from jax.experimental.pallas import tpu as pltpu
from jax.sharding import PartitionSpec as P

MIB = 1024 * 1024


def whole(space=pltpu.VMEM):
    return pl.BlockSpec(memory_space=space)


def cost(flops, moved):
    return pl.CostEstimate(flops=flops, bytes_accessed=moved, transcendentals=0)


def params(mib):
    return pltpu.CompilerParams(vmem_limit_bytes=mib * MIB)


def nesterov_kernel(plan, shards, where_ref, g_ref, m_ref, *outs):
    for out, pieces in zip(outs, plan):
        for i, (k, u) in enumerate(pieces):
            source = (where_ref[0] ^ k) * shards + (where_ref[1] ^ u)
            g = g_ref[source].astype(jnp.float32)
            m = 0.95 * m_ref[source] + g
            out[i] = (g + 0.95 * m).astype(jnp.bfloat16)


def nesterov(grads, momentum, where, plan, shards):
    count, rows, cols = grads.shape
    n = sum(len(pieces) for pieces in plan)
    return pl.pallas_call(
        functools.partial(nesterov_kernel, plan, shards),
        in_specs=[whole(pltpu.SMEM), whole(), whole()],
        out_specs=[whole()] * len(plan),
        out_shape=[jax.ShapeDtypeStruct((len(pieces), rows, cols), jnp.bfloat16) for pieces in plan],
        compiler_params=params(8),
        cost_estimate=cost(6 * n * rows * cols, 8 * n * rows * cols),
    )(where, grads, momentum)


def momentum_kernel(g_ref, m_ref, after_ref, o_ref, token_ref):
    o_ref[...] = 0.95 * m_ref[...] + g_ref[...].astype(jnp.float32)
    token_ref[...] = jnp.zeros_like(token_ref)


def next_momentum(grads, momentum, after):
    count, rows, cols = grads.shape
    steps = 8
    spec = pl.BlockSpec((count // steps, rows, cols), lambda i: (i, 0, 0))
    return pl.pallas_call(
        momentum_kernel,
        grid=(steps,),
        in_specs=[spec, spec, whole(pl.ANY)],
        out_specs=[spec, whole()],
        out_shape=[
            jax.ShapeDtypeStruct(grads.shape, jnp.float32),
            jax.ShapeDtypeStruct((8, 128), jnp.float32),
        ],
        compiler_params=params(8),
        cost_estimate=cost(1000, 1000),
    )(grads, momentum, after)


def nesterov_group(grads, momentum, group, shards):
    g = lax.dynamic_slice_in_dim(grads, group * shards, shards, 0).astype(jnp.float32)
    m = lax.dynamic_slice_in_dim(momentum, group * shards, shards, 0)
    return (g + 0.95 * (0.95 * m + g)).astype(jnp.bfloat16)


def plans(shards):
    z2 = [(2, u) for u in range(shards)]
    p31 = [[(3, u), (1, u)] for u in range(shards)]
    a0 = [(0, u) for u in range(shards)]
    return [z2], p31, [a0]


def swap_tensor(piece, k):
    count = lax.axis_size("tensor")
    return lax.ppermute(piece, "tensor", [(t, t ^ k) for t in range(count)])


def swap_shard(piece, u):
    count = lax.axis_size("shard")
    return lax.ppermute(piece, "shard", [(s, s ^ u) for s in range(count)])


def regroup_kernel(plan, n, where_ref, *refs):
    ins, outs = refs[:n], refs[n:]
    for out, slabs in zip(outs, plan):
        for i, (a, b, moved) in enumerate(slabs):
            out[i] = ins[a][b ^ where_ref[1] if moved else b]


def regroup(where, arrays, plan):
    _, rows, cols = arrays[0].shape
    n = sum(len(slabs) for slabs in plan)
    return pl.pallas_call(
        functools.partial(regroup_kernel, plan, len(arrays)),
        in_specs=[whole(pltpu.SMEM)] + [whole()] * len(arrays),
        out_specs=[whole()] * len(plan),
        out_shape=[jax.ShapeDtypeStruct((len(slabs), rows, cols), jnp.bfloat16) for slabs in plan],
        compiler_params=params(8),
        cost_estimate=cost(0, 4 * n * rows * cols),
    )(where, *arrays)


def exchange(where, z2, p31, a0, moved):
    shards = len(p31)
    z2 = swap_tensor(z2, 2)
    p31 = [p31[0]] + [swap_shard(p31[u], u) for u in range(1, shards)]
    w3, w1 = regroup(where, p31, [[(u, i, False) for u in range(shards)] for i in range(2)])
    z3 = swap_tensor(w3, 3)
    z1 = swap_tensor(w1, 1)
    p20 = regroup(where, (z2, a0), [[(0, u, moved), (1, u, False)] for u in range(shards)])
    p20 = [p20[0]] + [swap_shard(p20[u], u) for u in range(1, shards)]
    outs = {3: [(z3, u) for u in range(shards)], 1: [(z1, u) for u in range(shards)]}
    for i, k in enumerate((2, 0)):
        outs[k] = [(a, i) for a in p20]
    return outs


def arrays_of(chunks):
    arrays, places = [], []
    for k in sorted(chunks):
        for u, (a, b) in enumerate(chunks[k]):
            known = [i for i, other in enumerate(arrays) if other is a]
            if not known:
                known = [len(arrays)]
                arrays.append(a)
            places.append((k, u, known[0], b))
    return arrays, places


def mm(a, b):
    return jnp.dot(a, b, preferred_element_type=jnp.float32)


def mm_rows(a, b):
    return lax.dot_general(a, b, (((1,), (1,)), ((), ())), preferred_element_type=jnp.float32)


def step_columns(gram_ref, x, power_ref, scale):
    power = mm(gram_ref[...], x)
    if scale is not None:
        power = power * (scale * scale * scale)
    power_ref[...] = power
    square = mm(gram_ref[...], power.astype(jnp.bfloat16))
    current = x.astype(jnp.float32)
    if scale is not None:
        square = square * (scale * scale)
        current = current * scale
    return (3.4445 * current - 4.775 * power_ref[...] + 2.0315 * square).astype(jnp.bfloat16)


def gram_rows(x_ref, gram_ref, tile, with_trace):
    order = x_ref.shape[0]
    trace = jnp.zeros((tile, tile), jnp.float32)
    eye = lax.broadcasted_iota(jnp.int32, (tile, tile), 0) == lax.broadcasted_iota(jnp.int32, (tile, tile), 1)
    for i in range(order // tile):
        rows = slice(i * tile, (i + 1) * tile)
        part = mm_rows(x_ref[rows, :], x_ref[...])
        if with_trace:
            trace = trace + jnp.where(eye, part[:, rows], 0.0)
        gram_ref[rows, :] = part.astype(jnp.bfloat16)
    return jnp.sum(trace) if with_trace else None


def finish(new, k, plan, outs):
    rows = outs[0].shape[1]
    gain = 0.2 * float(new.shape[0]) ** 0.5
    done = (gain * new.astype(jnp.float32)).astype(jnp.bfloat16)
    for out, pieces in zip(outs, plan):
        for i, (k_of, u) in enumerate(pieces):
            if k_of == k:
                out[i] = done[u * rows : (u + 1) * rows]


def first_kernel(places, plan, n, *refs):
    ins, refs = refs[:n], refs[n + 1 :]
    y_ref, h_ref, refs = refs[0], refs[1], refs[2:]
    outs, (x_ref, g_ref, power_ref) = refs[: len(plan)], refs[len(plan) :]
    order, cols = power_ref.shape
    rows = ins[0].shape[1]
    for k, u, which, b in places:
        x_ref[u * rows : (u + 1) * rows, k * cols : (k + 1) * cols] = ins[which][b]
    tile = min(256, order)
    total = gram_rows(x_ref, g_ref, tile, True)
    scale = 1.0 / (jnp.sqrt(total) + 1e-07)
    for k in range(order // cols):
        c = slice(k * cols, (k + 1) * cols)
        y_ref[:, c] = step_columns(g_ref, x_ref[:, c], power_ref, scale)
    gram_rows(y_ref, h_ref, tile, False)
    for k in sorted({k for pieces in plan for k, _ in pieces}):
        new = step_columns(h_ref, y_ref[:, k * cols : (k + 1) * cols], power_ref, None)
        finish(new, k, plan, outs)


def first(chunks, plan, after):
    arrays, places = arrays_of(chunks)
    _, rows, cols = arrays[0].shape
    order = cols * len(chunks)
    square = jax.ShapeDtypeStruct((order, order), jnp.bfloat16)
    return pl.pallas_call(
        functools.partial(first_kernel, places, plan, len(arrays)),
        in_specs=[whole()] * len(arrays) + [whole(pl.ANY)],
        out_specs=[whole()] * (2 + len(plan)),
        out_shape=[square, square]
        + [jax.ShapeDtypeStruct((len(pieces), rows, cols), jnp.bfloat16) for pieces in plan],
        scratch_shapes=[pltpu.VMEM((order, order), jnp.bfloat16)] * 2 + [pltpu.VMEM((order, cols), jnp.float32)],
        compiler_params=params(24),
        cost_estimate=cost(9 * order**3, 12 * order**2),
    )(*arrays, after)


def last_kernel(plan, x_ref, g_ref, *refs):
    outs, power_ref = refs[:-1], refs[-1]
    order, cols = power_ref.shape
    for k in sorted({k for pieces in plan for k, _ in pieces}, reverse=True):
        new = step_columns(g_ref, x_ref[:, k * cols : (k + 1) * cols], power_ref, None)
        finish(new, k, plan, outs)


def last(x, g, plan, rows, cols):
    order = x.shape[0]
    return pl.pallas_call(
        functools.partial(last_kernel, plan),
        in_specs=[whole()] * 2,
        out_specs=[whole()] * len(plan),
        out_shape=[jax.ShapeDtypeStruct((len(pieces), rows, cols), jnp.bfloat16) for pieces in plan],
        scratch_shapes=[pltpu.VMEM((order, cols), jnp.float32)],
        compiler_params=params(16),
        cost_estimate=cost(len(plan) // 8 * order**3 + order**3, 8 * order**2),
    )(x, g)


def place_kernel(places, shards, where_ref, *refs):
    o_ref, sems = refs[-2:]
    copies = []
    for n, (k, u, which, b) in enumerate(places):
        target = (where_ref[0] ^ k) * shards + (where_ref[1] ^ u)
        copies.append(pltpu.make_async_copy(refs[which].at[b], o_ref.at[target], sems.at[n]))
    for c in copies:
        c.start()
    for c in copies:
        c.wait()


def place(where, chunks, shards, shape, before):
    arrays, places = arrays_of(chunks)
    more = [] if before is None else [before]
    return pl.pallas_call(
        functools.partial(place_kernel, places, shards),
        in_specs=[whole(pltpu.SMEM)] + [whole()] * len(arrays) + [whole(pltpu.HBM)] * len(more),
        out_specs=whole(pltpu.HBM),
        out_shape=jax.ShapeDtypeStruct(shape, jnp.bfloat16),
        scratch_shapes=[pltpu.SemaphoreType.DMA((len(places),))],
        input_output_aliases={len(arrays) + 1: 0} if more else {},
        compiler_params=params(8),
        cost_estimate=cost(0, 4 * len(places) * shape[1] * shape[2]),
    )(where, *arrays, *more)


def shards(grads, momentum):
    count, rows, cols = grads.shape
    shard_count = lax.axis_size("shard")
    t = lax.axis_index("tensor")
    where = jnp.stack([t, lax.axis_index("shard")]).astype(jnp.int32)
    z2_plan, p31_plan, a0_plan = plans(shard_count)
    z2 = nesterov_group(grads, momentum, t ^ 2, shard_count)
    p31 = nesterov(grads, momentum, where, p31_plan, shard_count)
    (a0,) = nesterov(grads, momentum, where, a0_plan, shard_count)
    chunks = exchange(where, z2, p31, a0, True)
    momentum_next, token = next_momentum(grads, momentum, chunks[0][0][0])
    x, g, z2 = first(chunks, z2_plan, token)
    p31 = list(last(x, g, p31_plan, rows, cols))
    (a0,) = last(x, g, a0_plan, rows, cols)
    back = exchange(where, z2, p31, a0, False)
    update = place(where, back, shard_count, grads.shape, None)
    return (momentum_next, update)


def solution(mesh):
    return jax.shard_map(
        shards,
        mesh=mesh,
        in_specs=(P(None, "shard", "tensor"), P(None, "shard", "tensor")),
        out_specs=(P(None, "shard", "tensor"), P(None, "shard", "tensor")),
        check_vma=False,
    )
```

```python
import functools

import jax
import jax.numpy as jnp
from jax import lax
from jax.experimental import pallas as pl
from jax.experimental.pallas import tpu as pltpu
from jax.sharding import PartitionSpec as P

MIB = 1024 * 1024


def whole(space=pltpu.VMEM):
    return pl.BlockSpec(memory_space=space)


def cost(flops, moved):
    return pl.CostEstimate(flops=flops, bytes_accessed=moved, transcendentals=0)


def params(mib):
    return pltpu.CompilerParams(vmem_limit_bytes=mib * MIB)


def nesterov_kernel(plan, shards, where_ref, g_ref, m_ref, *outs):
    for out, pieces in zip(outs, plan):
        for i, (k, u) in enumerate(pieces):
            source = (where_ref[0] ^ k) * shards + (where_ref[1] ^ u)
            g = g_ref[source].astype(jnp.float32)
            m = 0.95 * m_ref[source] + g
            out[i] = (g + 0.95 * m).astype(jnp.bfloat16)


def nesterov(grads, momentum, where, plan, shards):
    count, rows, cols = grads.shape
    n = sum(len(pieces) for pieces in plan)
    return pl.pallas_call(
        functools.partial(nesterov_kernel, plan, shards),
        in_specs=[whole(pltpu.SMEM), whole(), whole()],
        out_specs=[whole()] * len(plan),
        out_shape=[jax.ShapeDtypeStruct((len(pieces), rows, cols), jnp.bfloat16) for pieces in plan],
        compiler_params=params(8),
        cost_estimate=cost(6 * n * rows * cols, 8 * n * rows * cols),
    )(where, grads, momentum)


def momentum_kernel(g_ref, m_ref, after_ref, o_ref, token_ref):
    o_ref[...] = 0.95 * m_ref[...] + g_ref[...].astype(jnp.float32)
    token_ref[...] = jnp.zeros_like(token_ref)


def next_momentum(grads, momentum, after):
    count, rows, cols = grads.shape
    steps = 8
    spec = pl.BlockSpec((count // steps, rows, cols), lambda i: (i, 0, 0))
    return pl.pallas_call(
        momentum_kernel,
        grid=(steps,),
        in_specs=[spec, spec, whole(pl.ANY)],
        out_specs=[spec, whole()],
        out_shape=[
            jax.ShapeDtypeStruct(grads.shape, jnp.float32),
            jax.ShapeDtypeStruct((8, 128), jnp.float32),
        ],
        compiler_params=params(8),
        cost_estimate=cost(1000, 1000),
    )(grads, momentum, after)


def nesterov_group(grads, momentum, group, shards):
    g = lax.dynamic_slice_in_dim(grads, group * shards, shards, 0).astype(jnp.float32)
    m = lax.dynamic_slice_in_dim(momentum, group * shards, shards, 0)
    return (g + 0.95 * (0.95 * m + g)).astype(jnp.bfloat16)


def plans(shards):
    z2 = [(2, u) for u in range(shards)]
    p31 = [[(3, u), (1, u)] for u in range(shards)]
    a0 = [(0, u) for u in range(shards)]
    return [z2], p31, [a0]


def swap_tensor(piece, k):
    count = lax.axis_size("tensor")
    return lax.ppermute(piece, "tensor", [(t, t ^ k) for t in range(count)])


def swap_shard(piece, u):
    count = lax.axis_size("shard")
    return lax.ppermute(piece, "shard", [(s, s ^ u) for s in range(count)])


def regroup_kernel(plan, n, where_ref, *refs):
    ins, outs = refs[:n], refs[n:]
    for out, slabs in zip(outs, plan):
        for i, (a, b, moved, moves) in enumerate(slabs):
            out[i ^ where_ref[1] if moves else i] = ins[a][b ^ where_ref[1] if moved else b]


def regroup(where, arrays, plan):
    _, rows, cols = arrays[0].shape
    n = sum(len(slabs) for slabs in plan)
    return pl.pallas_call(
        functools.partial(regroup_kernel, plan, len(arrays)),
        in_specs=[whole(pltpu.SMEM)] + [whole()] * len(arrays),
        out_specs=[whole()] * len(plan),
        out_shape=[jax.ShapeDtypeStruct((len(slabs), rows, cols), jnp.bfloat16) for slabs in plan],
        compiler_params=params(8),
        cost_estimate=cost(0, 4 * n * rows * cols),
    )(where, *arrays)


def exchange(where, z2, p31, a0, moved):
    shards = len(p31)
    z2 = swap_tensor(z2, 2)
    p31 = [p31[0]] + [swap_shard(p31[u], u) for u in range(1, shards)]
    w3, w1 = regroup(where, p31, [[(u, i, False, not moved) for u in range(shards)] for i in range(2)])
    z3 = swap_tensor(w3, 3)
    z1 = swap_tensor(w1, 1)
    p20 = regroup(where, (z2, a0), [[(0, u, moved, False), (1, u, False, False)] for u in range(shards)])
    p20 = [p20[0]] + [swap_shard(p20[u], u) for u in range(1, shards)]
    outs = {k: [(a, i) for a in p20] for i, k in enumerate((2, 0))}
    for k, a in ((3, z3), (1, z1)):
        outs[k] = [(a, u) for u in range(shards)] if moved else [(a, None)]
    return outs


def arrays_of(chunks):
    arrays, places = [], []
    for k in sorted(chunks):
        for u, (a, b) in enumerate(chunks[k]):
            known = [i for i, other in enumerate(arrays) if other is a]
            if not known:
                known = [len(arrays)]
                arrays.append(a)
            places.append((k, u, known[0], b))
    return arrays, places


def mm(a, b):
    return jnp.dot(a, b, preferred_element_type=jnp.float32)


def mm_rows(a, b):
    return lax.dot_general(a, b, (((1,), (1,)), ((), ())), preferred_element_type=jnp.float32)


def symmetric(x_ref, out_ref, with_trace=False, finish=None):
    order = x_ref.shape[0]
    tile = min(256, order)
    trace = jnp.zeros((tile, tile), jnp.float32)
    eye = lax.broadcasted_iota(jnp.int32, (tile, tile), 0) == lax.broadcasted_iota(jnp.int32, (tile, tile), 1)
    for i in range(order // tile):
        cols = slice(i * tile, (i + 1) * tile)
        below = slice(i * tile, order)
        part = mm_rows(x_ref[below, :], x_ref[cols, :])
        if with_trace:
            trace = trace + jnp.where(eye, part[:tile], 0.0)
        if finish is not None:
            part = finish(part, below, cols)
        part = part.astype(jnp.bfloat16)
        out_ref[below, cols] = part
        if i + 1 < order // tile:
            out_ref[cols, (i + 1) * tile :] = part[tile:].T
    return jnp.sum(trace) if with_trace else None


def step_columns(gram_ref, x, power_ref):
    power = mm(gram_ref[...], x)
    power_ref[...] = power
    square = mm(gram_ref[...], power.astype(jnp.bfloat16))
    return 3.4445 * x.astype(jnp.float32) - 4.775 * power_ref[...] + 2.0315 * square


def finish(new, k, plan, outs):
    rows = outs[0].shape[1]
    gain = 0.2 * float(new.shape[0]) ** 0.5
    done = (gain * new.astype(jnp.float32)).astype(jnp.bfloat16)
    for out, pieces in zip(outs, plan):
        for i, (k_of, u) in enumerate(pieces):
            if k_of == k:
                out[i] = done[u * rows : (u + 1) * rows]


def first_kernel(places, plan, n, *refs):
    ins, refs = refs[:n], refs[n + 1 :]
    y_ref, h_ref, refs = refs[0], refs[1], refs[2:]
    outs, (x_ref, g_ref, w_ref, power_ref) = refs[: len(plan)], refs[len(plan) :]
    order, cols = power_ref.shape
    rows = ins[0].shape[1]
    for k, u, which, b in places:
        x_ref[u * rows : (u + 1) * rows, k * cols : (k + 1) * cols] = ins[which][b]
    scale = 1.0 / (jnp.sqrt(symmetric(x_ref, g_ref, with_trace=True)) + 1e-07)
    by_gram, by_square = -4.775 * (scale * scale), 2.0315 * (scale * scale) * (scale * scale)

    def weights(square, rows, cols):
        return by_gram * g_ref[rows, cols].astype(jnp.float32) + by_square * square

    symmetric(g_ref, w_ref, finish=weights)
    for k in range(order // cols):
        c = slice(k * cols, (k + 1) * cols)
        x = x_ref[:, c]
        y_ref[:, c] = (scale * (3.4445 * x.astype(jnp.float32) + mm(w_ref[...], x))).astype(jnp.bfloat16)
    symmetric(y_ref, h_ref)
    for k in sorted({k for pieces in plan for k, _ in pieces}):
        new = step_columns(h_ref, y_ref[:, k * cols : (k + 1) * cols], power_ref)
        finish(new.astype(jnp.bfloat16), k, plan, outs)


def first(chunks, plan, after):
    arrays, places = arrays_of(chunks)
    _, rows, cols = arrays[0].shape
    order = cols * len(chunks)
    square = jax.ShapeDtypeStruct((order, order), jnp.bfloat16)
    return pl.pallas_call(
        functools.partial(first_kernel, places, plan, len(arrays)),
        in_specs=[whole()] * len(arrays) + [whole(pl.ANY)],
        out_specs=[whole()] * (2 + len(plan)),
        out_shape=[square, square]
        + [jax.ShapeDtypeStruct((len(pieces), rows, cols), jnp.bfloat16) for pieces in plan],
        scratch_shapes=[pltpu.VMEM((order, order), jnp.bfloat16)] * 3 + [pltpu.VMEM((order, cols), jnp.float32)],
        compiler_params=params(24),
        cost_estimate=cost(7 * order**3, 12 * order**2),
    )(*arrays, after)


def last_kernel(plan, x_ref, g_ref, *refs):
    outs, power_ref = refs[:-1], refs[-1]
    order, cols = power_ref.shape
    for k in sorted({k for pieces in plan for k, _ in pieces}, reverse=True):
        new = step_columns(g_ref, x_ref[:, k * cols : (k + 1) * cols], power_ref)
        finish(new.astype(jnp.bfloat16), k, plan, outs)


def last(x, g, plan, rows, cols):
    order = x.shape[0]
    return pl.pallas_call(
        functools.partial(last_kernel, plan),
        in_specs=[whole()] * 2,
        out_specs=[whole()] * len(plan),
        out_shape=[jax.ShapeDtypeStruct((len(pieces), rows, cols), jnp.bfloat16) for pieces in plan],
        scratch_shapes=[pltpu.VMEM((order, cols), jnp.float32)],
        compiler_params=params(16),
        cost_estimate=cost(len(plan) // 8 * order**3 + order**3, 8 * order**2),
    )(x, g)


def place_kernel(places, shards, where_ref, *refs):
    o_ref, sems = refs[-2:]
    copies = []
    for n, (k, u, which, b) in enumerate(places):
        group = (where_ref[0] ^ k) * shards
        if b is None:
            src, dst = refs[which], o_ref.at[pl.ds(group, shards)]
        else:
            src, dst = refs[which].at[b], o_ref.at[group + (where_ref[1] ^ u)]
        copies.append(pltpu.make_async_copy(src, dst, sems.at[n]))
    for c in copies:
        c.start()
    for c in copies:
        c.wait()


def place(where, chunks, shards, shape, before):
    arrays, places = arrays_of(chunks)
    more = [] if before is None else [before]
    return pl.pallas_call(
        functools.partial(place_kernel, places, shards),
        in_specs=[whole(pltpu.SMEM)] + [whole()] * len(arrays) + [whole(pltpu.HBM)] * len(more),
        out_specs=whole(pltpu.HBM),
        out_shape=jax.ShapeDtypeStruct(shape, jnp.bfloat16),
        scratch_shapes=[pltpu.SemaphoreType.DMA((len(places),))],
        input_output_aliases={len(arrays) + 1: 0} if more else {},
        compiler_params=params(8),
        cost_estimate=cost(0, 4 * shape[0] * shape[1] * shape[2]),
    )(where, *arrays, *more)


def shards(grads, momentum):
    count, rows, cols = grads.shape
    shard_count = lax.axis_size("shard")
    t = lax.axis_index("tensor")
    where = jnp.stack([t, lax.axis_index("shard")]).astype(jnp.int32)
    z2_plan, p31_plan, a0_plan = plans(shard_count)
    z2 = nesterov_group(grads, momentum, t ^ 2, shard_count)
    p31 = nesterov(grads, momentum, where, p31_plan, shard_count)
    (a0,) = nesterov(grads, momentum, where, a0_plan, shard_count)
    chunks = exchange(where, z2, p31, a0, True)
    momentum_next, token = next_momentum(grads, momentum, chunks[0][0][0])
    x, g, z2 = first(chunks, z2_plan, token)
    p31 = list(last(x, g, p31_plan, rows, cols))
    (a0,) = last(x, g, a0_plan, rows, cols)
    back = exchange(where, z2, p31, a0, False)
    update = place(where, back, shard_count, grads.shape, None)
    return (momentum_next, update)


def solution(mesh):
    return jax.shard_map(
        shards,
        mesh=mesh,
        in_specs=(P(None, "shard", "tensor"), P(None, "shard", "tensor")),
        out_specs=(P(None, "shard", "tensor"), P(None, "shard", "tensor")),
        check_vma=False,
    )
```

```python
import functools

import jax
import jax.numpy as jnp
from jax import lax
from jax.experimental import pallas as pl
from jax.experimental.pallas import tpu as pltpu
from jax.sharding import PartitionSpec as P

MIB = 1024 * 1024


def whole(space=pltpu.VMEM):
    return pl.BlockSpec(memory_space=space)


def cost(flops, moved):
    return pl.CostEstimate(flops=flops, bytes_accessed=moved, transcendentals=0)


def params(mib):
    return pltpu.CompilerParams(vmem_limit_bytes=mib * MIB)


def nesterov_kernel(plan, shards, where_ref, g_ref, m_ref, *outs):
    for out, pieces in zip(outs, plan):
        for i, (k, u) in enumerate(pieces):
            source = (where_ref[0] ^ k) * shards + (where_ref[1] ^ u)
            g = g_ref[source].astype(jnp.float32)
            m = 0.95 * m_ref[source] + g
            out[i] = (g + 0.95 * m).astype(jnp.bfloat16)


def nesterov(grads, momentum, where, plan, shards):
    count, rows, cols = grads.shape
    n = sum(len(pieces) for pieces in plan)
    return pl.pallas_call(
        functools.partial(nesterov_kernel, plan, shards),
        in_specs=[whole(pltpu.SMEM), whole(), whole()],
        out_specs=[whole()] * len(plan),
        out_shape=[jax.ShapeDtypeStruct((len(pieces), rows, cols), jnp.bfloat16) for pieces in plan],
        compiler_params=params(8),
        cost_estimate=cost(6 * n * rows * cols, 8 * n * rows * cols),
    )(where, grads, momentum)


def momentum_kernel(g_ref, m_ref, after_ref, o_ref, token_ref):
    o_ref[...] = 0.95 * m_ref[...] + g_ref[...].astype(jnp.float32)
    token_ref[...] = jnp.zeros_like(token_ref)


def next_momentum(grads, momentum, after):
    count, rows, cols = grads.shape
    steps = 8
    spec = pl.BlockSpec((count // steps, rows, cols), lambda i: (i, 0, 0))
    return pl.pallas_call(
        momentum_kernel,
        grid=(steps,),
        in_specs=[spec, spec, whole(pl.ANY)],
        out_specs=[spec, whole()],
        out_shape=[
            jax.ShapeDtypeStruct(grads.shape, jnp.float32),
            jax.ShapeDtypeStruct((8, 128), jnp.float32),
        ],
        compiler_params=params(8),
        cost_estimate=cost(1000, 1000),
    )(grads, momentum, after)


def nesterov_group(grads, momentum, group, shards):
    g = lax.dynamic_slice_in_dim(grads, group * shards, shards, 0).astype(jnp.float32)
    m = lax.dynamic_slice_in_dim(momentum, group * shards, shards, 0)
    return (g + 0.95 * (0.95 * m + g)).astype(jnp.bfloat16)


def plans(shards):
    z2 = [(2, u) for u in range(shards)]
    p31 = [[(3, u), (1, u)] for u in range(shards)]
    a0 = [(0, u) for u in range(shards)]
    return [z2], p31, [a0]


def swap_tensor(piece, k):
    count = lax.axis_size("tensor")
    return lax.ppermute(piece, "tensor", [(t, t ^ k) for t in range(count)])


def swap_shard(piece, u):
    count = lax.axis_size("shard")
    return lax.ppermute(piece, "shard", [(s, s ^ u) for s in range(count)])


def regroup_kernel(plan, n, where_ref, *refs):
    ins, outs = refs[:n], refs[n:]
    for out, slabs in zip(outs, plan):
        for i, (a, b, moved, moves) in enumerate(slabs):
            out[i ^ where_ref[1] if moves else i] = ins[a][b ^ where_ref[1] if moved else b]


def regroup(where, arrays, plan):
    _, rows, cols = arrays[0].shape
    n = sum(len(slabs) for slabs in plan)
    return pl.pallas_call(
        functools.partial(regroup_kernel, plan, len(arrays)),
        in_specs=[whole(pltpu.SMEM)] + [whole()] * len(arrays),
        out_specs=[whole()] * len(plan),
        out_shape=[jax.ShapeDtypeStruct((len(slabs), rows, cols), jnp.bfloat16) for slabs in plan],
        compiler_params=params(8),
        cost_estimate=cost(0, 4 * n * rows * cols),
    )(where, *arrays)


def exchange(where, z2, p31, a0, moved):
    shards = len(p31)
    z2 = swap_tensor(z2, 2)
    p31 = [p31[0]] + [swap_shard(p31[u], u) for u in range(1, shards)]
    w3, w1 = regroup(where, p31, [[(u, i, False, not moved) for u in range(shards)] for i in range(2)])
    z3 = swap_tensor(w3, 3)
    z1 = swap_tensor(w1, 1)
    p20 = regroup(where, (z2, a0), [[(0, u, moved, False), (1, u, False, False)] for u in range(shards)])
    p20 = [p20[0]] + [swap_shard(p20[u], u) for u in range(1, shards)]
    outs = {k: [(a, i) for a in p20] for i, k in enumerate((2, 0))}
    for k, a in ((3, z3), (1, z1)):
        outs[k] = [(a, u) for u in range(shards)] if moved else [(a, None)]
    return outs


def arrays_of(chunks):
    arrays, places = [], []
    for k in sorted(chunks):
        for u, (a, b) in enumerate(chunks[k]):
            known = [i for i, other in enumerate(arrays) if other is a]
            if not known:
                known = [len(arrays)]
                arrays.append(a)
            places.append((k, u, known[0], b))
    return arrays, places


def mm(a, b):
    return jnp.dot(a, b, preferred_element_type=jnp.float32)


def mm_rows(a, b):
    return lax.dot_general(a, b, (((1,), (1,)), ((), ())), preferred_element_type=jnp.float32)


def symmetric(x_ref, out_ref, with_trace=False, finish=None, mirror=True):
    order = x_ref.shape[0]
    tile = min(256, order)
    trace = jnp.zeros((tile, tile), jnp.float32)
    eye = lax.broadcasted_iota(jnp.int32, (tile, tile), 0) == lax.broadcasted_iota(jnp.int32, (tile, tile), 1)
    for i in range(order // tile):
        cols = slice(i * tile, (i + 1) * tile)
        below = slice(i * tile, order)
        part = mm_rows(x_ref[below, :], x_ref[cols, :])
        if finish is not None:
            part = finish(part, below, cols)
        if with_trace:
            trace = trace + jnp.where(eye, part[:tile], 0.0)
        part = part.astype(out_ref.dtype)
        out_ref[below, cols] = part
        if mirror and i + 1 < order // tile:
            out_ref[cols, (i + 1) * tile :] = part[tile:].T
    return jnp.sum(trace) if with_trace else None


def step_columns(gram_ref, x, power_ref):
    power = mm(gram_ref[...], x)
    power_ref[...] = power
    square = mm(gram_ref[...], power.astype(jnp.bfloat16))
    return 3.4445 * x.astype(jnp.float32) - 4.775 * power_ref[...] + 2.0315 * square


def finish(new, k, plan, outs):
    rows = outs[0].shape[1]
    gain = 0.2 * float(new.shape[0]) ** 0.5
    done = (gain * new.astype(jnp.float32)).astype(jnp.bfloat16)
    for out, pieces in zip(outs, plan):
        for i, (k_of, u) in enumerate(pieces):
            if k_of == k:
                out[i] = done[u * rows : (u + 1) * rows]


def early_kernel(places, n, *refs):
    ins, (x_ref, part_ref) = refs[:n], refs[n:]
    rows, cols = ins[0].shape[1:]
    at = {k: i * cols for i, k in enumerate(sorted({p[0] for p in places}))}
    for k, u, which, b in places:
        x_ref[u * rows : (u + 1) * rows, at[k] : at[k] + cols] = ins[which][b]
    symmetric(x_ref, part_ref, mirror=False)


def early(chunks):
    arrays, places = arrays_of(chunks)
    _, rows, cols = arrays[0].shape
    order = rows * len(chunks[0])
    return pl.pallas_call(
        functools.partial(early_kernel, places, len(arrays)),
        in_specs=[whole()] * len(arrays),
        out_specs=[whole()] * 2,
        out_shape=[
            jax.ShapeDtypeStruct((order, cols * len(chunks)), jnp.bfloat16),
            jax.ShapeDtypeStruct((order, order), jnp.float32),
        ],
        compiler_params=params(16),
        cost_estimate=cost(1000, 1000),
    )(*arrays)


def first_kernel(early_ks, late_ks, plan, *refs):
    before_ref, part_ref, refs = refs[0], refs[1], refs[2:]
    late_refs, (y_ref, h_ref), refs = refs[: len(late_ks)], refs[len(late_ks) + 1 :][:2], refs[len(late_ks) + 3 :]
    outs, (x_ref, g_ref, w_ref, power_ref) = refs[: len(plan)], refs[len(plan) :]
    order, cols = power_ref.shape
    where = {}
    for i, (k, ref) in enumerate(zip(late_ks, late_refs)):
        where[k] = (x_ref, slice(i * cols, (i + 1) * cols))
        x_ref[:, i * cols : (i + 1) * cols] = ref[...].reshape(order, cols)
    for i, k in enumerate(early_ks):
        where[k] = (before_ref, slice(i * cols, (i + 1) * cols))

    def chunk(k):
        ref, c = where[k]
        return ref[:, c]

    def add(part, rows, cols):
        return part + part_ref[rows, cols]

    scale = 1.0 / (jnp.sqrt(symmetric(x_ref, g_ref, with_trace=True, finish=add)) + 1e-07)
    by_gram, by_square = -4.775 * (scale * scale), 2.0315 * (scale * scale) * (scale * scale)

    def weights(square, rows, cols):
        return by_gram * g_ref[rows, cols].astype(jnp.float32) + by_square * square

    symmetric(g_ref, w_ref, finish=weights)
    for k in range(order // cols):
        c = slice(k * cols, (k + 1) * cols)
        x = chunk(k)
        y_ref[:, c] = (scale * (3.4445 * x.astype(jnp.float32) + mm(w_ref[...], x))).astype(jnp.bfloat16)
    symmetric(y_ref, h_ref)
    for k in sorted({k for pieces in plan for k, _ in pieces}):
        new = step_columns(h_ref, y_ref[:, k * cols : (k + 1) * cols], power_ref)
        finish(new.astype(jnp.bfloat16), k, plan, outs)


def first(early_ks, before, part, late, plan, after):
    shards, rows, cols = late[max(late)].shape
    order = shards * rows
    late_ks = sorted(late)
    square = jax.ShapeDtypeStruct((order, order), jnp.bfloat16)
    return pl.pallas_call(
        functools.partial(first_kernel, early_ks, late_ks, plan),
        in_specs=[whole()] * (2 + len(late)) + [whole(pl.ANY)],
        out_specs=[whole()] * (2 + len(plan)),
        out_shape=[square, square]
        + [jax.ShapeDtypeStruct((len(pieces), rows, cols), jnp.bfloat16) for pieces in plan],
        scratch_shapes=[pltpu.VMEM((order, len(late) * cols), jnp.bfloat16)]
        + [pltpu.VMEM((order, order), jnp.bfloat16)] * 2
        + [pltpu.VMEM((order, cols), jnp.float32)],
        compiler_params=params(20),
        cost_estimate=cost(7 * order**3, 12 * order**2),
    )(before, part, *[late[k] for k in late_ks], after)


def last_kernel(plan, x_ref, g_ref, *refs):
    outs, power_ref = refs[:-1], refs[-1]
    order, cols = power_ref.shape
    for k in sorted({k for pieces in plan for k, _ in pieces}, reverse=True):
        new = step_columns(g_ref, x_ref[:, k * cols : (k + 1) * cols], power_ref)
        finish(new.astype(jnp.bfloat16), k, plan, outs)


def last(x, g, plan, rows, cols):
    order = x.shape[0]
    return pl.pallas_call(
        functools.partial(last_kernel, plan),
        in_specs=[whole()] * 2,
        out_specs=[whole()] * len(plan),
        out_shape=[jax.ShapeDtypeStruct((len(pieces), rows, cols), jnp.bfloat16) for pieces in plan],
        scratch_shapes=[pltpu.VMEM((order, cols), jnp.float32)],
        compiler_params=params(16),
        cost_estimate=cost(len(plan) // 8 * order**3 + order**3, 8 * order**2),
    )(x, g)


def place_kernel(places, shards, where_ref, *refs):
    o_ref, sems = refs[-2:]
    copies = []
    for n, (k, u, which, b) in enumerate(places):
        group = (where_ref[0] ^ k) * shards
        if b is None:
            src, dst = refs[which], o_ref.at[pl.ds(group, shards)]
        else:
            src, dst = refs[which].at[b], o_ref.at[group + (where_ref[1] ^ u)]
        copies.append(pltpu.make_async_copy(src, dst, sems.at[n]))
    for c in copies:
        c.start()
    for c in copies:
        c.wait()


def place(where, chunks, shards, shape, before):
    arrays, places = arrays_of(chunks)
    more = [] if before is None else [before]
    return pl.pallas_call(
        functools.partial(place_kernel, places, shards),
        in_specs=[whole(pltpu.SMEM)] + [whole()] * len(arrays) + [whole(pltpu.HBM)] * len(more),
        out_specs=whole(pltpu.HBM),
        out_shape=jax.ShapeDtypeStruct(shape, jnp.bfloat16),
        scratch_shapes=[pltpu.SemaphoreType.DMA((len(places),))],
        input_output_aliases={len(arrays) + 1: 0} if more else {},
        compiler_params=params(8),
        cost_estimate=cost(1000, 1000),
    )(where, *arrays, *more)


def shards(grads, momentum):
    count, rows, cols = grads.shape
    shard_count = lax.axis_size("shard")
    t = lax.axis_index("tensor")
    where = jnp.stack([t, lax.axis_index("shard")]).astype(jnp.int32)
    z2_plan, p31_plan, a0_plan = plans(shard_count)
    z2 = nesterov_group(grads, momentum, t ^ 2, shard_count)
    z2, grads, momentum = lax.optimization_barrier((z2, grads, momentum))
    p31 = nesterov(grads, momentum, where, p31_plan, shard_count)
    (a0,) = nesterov(grads, momentum, where, a0_plan, shard_count)
    chunks = exchange(where, z2, p31, a0, True)
    momentum_next, token = next_momentum(grads, momentum, chunks[0][0][0])
    before, part = early({k: chunks[k] for k in (0, 2)})
    x, g, z2 = first((0, 2), before, part, {k: chunks[k][0][0] for k in (1, 3)}, z2_plan, token)
    p31 = list(last(x, g, p31_plan, rows, cols))
    (a0,) = last(x, g, a0_plan, rows, cols)
    back = exchange(where, z2, p31, a0, False)
    update = place(where, {k: back[k] for k in (0, 2)}, shard_count, grads.shape, None)
    update = place(where, {k: back[k] for k in (1, 3)}, shard_count, grads.shape, update)
    return (momentum_next, update)


def solution(mesh):
    return jax.shard_map(
        shards,
        mesh=mesh,
        in_specs=(P(None, "shard", "tensor"), P(None, "shard", "tensor")),
        out_specs=(P(None, "shard", "tensor"), P(None, "shard", "tensor")),
        check_vma=False,
    )
```

```python
import functools

import jax
import jax.numpy as jnp
from jax import lax
from jax.experimental import pallas as pl
from jax.experimental.pallas import tpu as pltpu
from jax.sharding import PartitionSpec as P

MIB = 1024 * 1024


def whole(space=pltpu.VMEM):
    return pl.BlockSpec(memory_space=space)


def cost(flops, moved):
    return pl.CostEstimate(flops=flops, bytes_accessed=moved, transcendentals=0)


def params(mib):
    return pltpu.CompilerParams(vmem_limit_bytes=mib * MIB)


def nesterov_kernel(plan, shards, g_ref, m_ref, *outs):
    t, s = lax.axis_index("tensor"), lax.axis_index("shard")
    for out, pieces in zip(outs, plan):
        for i, (k, u) in enumerate(pieces):
            source = (t ^ k) * shards + (s ^ u)
            g = g_ref[source].astype(jnp.float32)
            m = 0.95 * m_ref[source] + g
            out[i] = (g + 0.95 * m).astype(jnp.bfloat16)


def nesterov(grads, momentum, plan, shards):
    count, rows, cols = grads.shape
    n = sum(len(pieces) for pieces in plan)
    return pl.pallas_call(
        functools.partial(nesterov_kernel, plan, shards),
        in_specs=[whole(), whole()],
        out_specs=[whole()] * len(plan),
        out_shape=[jax.ShapeDtypeStruct((len(pieces), rows, cols), jnp.bfloat16) for pieces in plan],
        compiler_params=params(8),
        cost_estimate=cost(6 * n * rows * cols, 8 * n * rows * cols),
    )(grads, momentum)


def momentum_kernel(g_ref, m_ref, after_ref, o_ref, token_ref):
    o_ref[...] = 0.95 * m_ref[...] + g_ref[...].astype(jnp.float32)
    token_ref[...] = jnp.zeros_like(token_ref)


def next_momentum(grads, momentum, after):
    count, rows, cols = grads.shape
    steps = 8
    spec = pl.BlockSpec((count // steps, rows, cols), lambda i: (i, 0, 0))
    return pl.pallas_call(
        momentum_kernel,
        grid=(steps,),
        in_specs=[spec, spec, whole(pl.ANY)],
        out_specs=[spec, whole()],
        out_shape=[
            jax.ShapeDtypeStruct(grads.shape, jnp.float32),
            jax.ShapeDtypeStruct((8, 128), jnp.float32),
        ],
        compiler_params=params(8),
        cost_estimate=cost(1000, 1000),
    )(grads, momentum, after)


def nesterov_group(grads, momentum, group, shards):
    g = lax.dynamic_slice_in_dim(grads, group * shards, shards, 0).astype(jnp.float32)
    m = lax.dynamic_slice_in_dim(momentum, group * shards, shards, 0)
    return (g + 0.95 * (0.95 * m + g)).astype(jnp.bfloat16)


def plans(shards):
    z2 = [(2, u) for u in range(shards)]
    p31 = [[(3, u), (1, u)] for u in range(shards)]
    a0 = [(0, u) for u in range(shards)]
    return [z2], p31, [a0]


def swap_tensor(piece, k):
    count = lax.axis_size("tensor")
    return lax.ppermute(piece, "tensor", [(t, t ^ k) for t in range(count)])


def swap_shard(piece, u):
    count = lax.axis_size("shard")
    return lax.ppermute(piece, "shard", [(s, s ^ u) for s in range(count)])


def regroup_kernel(plan, n, *refs):
    ins, outs = refs[:n], refs[n:]
    s = lax.axis_index("shard")
    for out, slabs in zip(outs, plan):
        for i, (a, b, moved, moves) in enumerate(slabs):
            out[i ^ s if moves else i] = ins[a][b ^ s if moved else b]


def regroup(arrays, plan):
    _, rows, cols = arrays[0].shape
    n = sum(len(slabs) for slabs in plan)
    return pl.pallas_call(
        functools.partial(regroup_kernel, plan, len(arrays)),
        in_specs=[whole()] * len(arrays),
        out_specs=[whole()] * len(plan),
        out_shape=[jax.ShapeDtypeStruct((len(slabs), rows, cols), jnp.bfloat16) for slabs in plan],
        compiler_params=params(8),
        cost_estimate=cost(0, 4 * n * rows * cols),
    )(*arrays)


def exchange(z2, p31, a0, moved):
    shards = len(p31)
    z2 = swap_tensor(z2, 2)
    p31 = [p31[0]] + [swap_shard(p31[u], u) for u in range(1, shards)]
    w3, w1 = regroup(p31, [[(u, i, False, not moved) for u in range(shards)] for i in range(2)])
    z3 = swap_tensor(w3, 3)
    z1 = swap_tensor(w1, 1)
    p20 = regroup((z2, a0), [[(0, u, moved, False), (1, u, False, False)] for u in range(shards)])
    p20 = [p20[0]] + [swap_shard(p20[u], u) for u in range(1, shards)]
    outs = {k: [(a, i) for a in p20] for i, k in enumerate((2, 0))}
    for k, a in ((3, z3), (1, z1)):
        outs[k] = [(a, u) for u in range(shards)] if moved else [(a, None)]
    return outs


def arrays_of(chunks):
    arrays, places = [], []
    for k in sorted(chunks):
        for u, (a, b) in enumerate(chunks[k]):
            known = [i for i, other in enumerate(arrays) if other is a]
            if not known:
                known = [len(arrays)]
                arrays.append(a)
            places.append((k, u, known[0], b))
    return arrays, places


def mm(a, b):
    return jnp.dot(a, b, preferred_element_type=jnp.float32)


def mm_rows(a, b):
    return lax.dot_general(a, b, (((1,), (1,)), ((), ())), preferred_element_type=jnp.float32)


def symmetric(x_ref, out_ref, with_trace=False, finish=None, mirror=True):
    order = x_ref.shape[0]
    tile = min(256, order)
    trace = jnp.zeros((tile, tile), jnp.float32)
    eye = lax.broadcasted_iota(jnp.int32, (tile, tile), 0) == lax.broadcasted_iota(jnp.int32, (tile, tile), 1)
    for i in range(order // tile):
        cols = slice(i * tile, (i + 1) * tile)
        below = slice(i * tile, order)
        part = mm_rows(x_ref[below, :], x_ref[cols, :])
        if finish is not None:
            part = finish(part, below, cols)
        if with_trace:
            trace = trace + jnp.where(eye, part[:tile], 0.0)
        part = part.astype(out_ref.dtype)
        out_ref[below, cols] = part
        if mirror and i + 1 < order // tile:
            out_ref[cols, (i + 1) * tile :] = part[tile:].T
    return jnp.sum(trace) if with_trace else None


def step_columns(gram_ref, x, power_ref):
    power = mm(gram_ref[...], x)
    power_ref[...] = power
    square = mm(gram_ref[...], power.astype(jnp.bfloat16))
    return 3.4445 * x.astype(jnp.float32) - 4.775 * power_ref[...] + 2.0315 * square


def finish(new, k, plan, outs):
    rows = outs[0].shape[1]
    gain = 0.2 * float(new.shape[0]) ** 0.5
    done = (gain * new.astype(jnp.float32)).astype(jnp.bfloat16)
    for out, pieces in zip(outs, plan):
        for i, (k_of, u) in enumerate(pieces):
            if k_of == k:
                out[i] = done[u * rows : (u + 1) * rows]


def early_kernel(places, n, *refs):
    ins, (x_ref, part_ref) = refs[:n], refs[n:]
    rows, cols = ins[0].shape[1:]
    at = {k: i * cols for i, k in enumerate(sorted({p[0] for p in places}))}
    for k, u, which, b in places:
        x_ref[u * rows : (u + 1) * rows, at[k] : at[k] + cols] = ins[which][b]
    symmetric(x_ref, part_ref, mirror=False)


def early(chunks):
    arrays, places = arrays_of(chunks)
    _, rows, cols = arrays[0].shape
    order = rows * len(chunks[0])
    return pl.pallas_call(
        functools.partial(early_kernel, places, len(arrays)),
        in_specs=[whole()] * len(arrays),
        out_specs=[whole()] * 2,
        out_shape=[
            jax.ShapeDtypeStruct((order, cols * len(chunks)), jnp.bfloat16),
            jax.ShapeDtypeStruct((order, order), jnp.float32),
        ],
        compiler_params=params(16),
        cost_estimate=cost(1000, 1000),
    )(*arrays)


def first_kernel(early_ks, late_ks, plan, *refs):
    before_ref, part_ref, refs = refs[0], refs[1], refs[2:]
    late_refs, (y_ref, h_ref), refs = refs[: len(late_ks)], refs[len(late_ks) + 1 :][:2], refs[len(late_ks) + 3 :]
    outs, (x_ref, g_ref, w_ref, power_ref) = refs[: len(plan)], refs[len(plan) :]
    order, cols = power_ref.shape
    where = {}
    for i, (k, ref) in enumerate(zip(late_ks, late_refs)):
        where[k] = (x_ref, slice(i * cols, (i + 1) * cols))
        x_ref[:, i * cols : (i + 1) * cols] = ref[...].reshape(order, cols)
    for i, k in enumerate(early_ks):
        where[k] = (before_ref, slice(i * cols, (i + 1) * cols))

    def chunk(k):
        ref, c = where[k]
        return ref[:, c]

    def add(part, rows, cols):
        return part + part_ref[rows, cols]

    scale = 1.0 / (jnp.sqrt(symmetric(x_ref, g_ref, with_trace=True, finish=add)) + 1e-07)
    by_gram, by_square = -4.775 * (scale * scale), 2.0315 * (scale * scale) * (scale * scale)

    def weights(square, rows, cols):
        return by_gram * g_ref[rows, cols].astype(jnp.float32) + by_square * square

    symmetric(g_ref, w_ref, finish=weights)
    for k in range(order // cols):
        c = slice(k * cols, (k + 1) * cols)
        x = chunk(k)
        y_ref[:, c] = (scale * (3.4445 * x.astype(jnp.float32) + mm(w_ref[...], x))).astype(jnp.bfloat16)
    symmetric(y_ref, h_ref)
    for k in sorted({k for pieces in plan for k, _ in pieces}):
        new = step_columns(h_ref, y_ref[:, k * cols : (k + 1) * cols], power_ref)
        finish(new.astype(jnp.bfloat16), k, plan, outs)


def first(early_ks, before, part, late, plan, after):
    shards, rows, cols = late[max(late)].shape
    order = shards * rows
    late_ks = sorted(late)
    square = jax.ShapeDtypeStruct((order, order), jnp.bfloat16)
    return pl.pallas_call(
        functools.partial(first_kernel, early_ks, late_ks, plan),
        in_specs=[whole()] * (2 + len(late)) + [whole(pl.ANY)],
        out_specs=[whole()] * (2 + len(plan)),
        out_shape=[square, square]
        + [jax.ShapeDtypeStruct((len(pieces), rows, cols), jnp.bfloat16) for pieces in plan],
        scratch_shapes=[pltpu.VMEM((order, len(late) * cols), jnp.bfloat16)]
        + [pltpu.VMEM((order, order), jnp.bfloat16)] * 2
        + [pltpu.VMEM((order, cols), jnp.float32)],
        compiler_params=params(20),
        cost_estimate=cost(7 * order**3, 12 * order**2),
    )(before, part, *[late[k] for k in late_ks], after)


def last_kernel(plan, x_ref, g_ref, *refs):
    outs, power_ref = refs[:-1], refs[-1]
    order, cols = power_ref.shape
    for k in sorted({k for pieces in plan for k, _ in pieces}, reverse=True):
        new = step_columns(g_ref, x_ref[:, k * cols : (k + 1) * cols], power_ref)
        finish(new.astype(jnp.bfloat16), k, plan, outs)


def last(x, g, plan, rows, cols):
    order = x.shape[0]
    return pl.pallas_call(
        functools.partial(last_kernel, plan),
        in_specs=[whole()] * 2,
        out_specs=[whole()] * len(plan),
        out_shape=[jax.ShapeDtypeStruct((len(pieces), rows, cols), jnp.bfloat16) for pieces in plan],
        scratch_shapes=[pltpu.VMEM((order, cols), jnp.float32)],
        compiler_params=params(16),
        cost_estimate=cost(len(plan) // 8 * order**3 + order**3, 8 * order**2),
    )(x, g)


def place_kernel(places, shards, *refs):
    o_ref, sems = refs[-2:]
    t, s = lax.axis_index("tensor"), lax.axis_index("shard")
    copies = []
    for n, (k, u, which, b) in enumerate(places):
        group = (t ^ k) * shards
        if b is None:
            src, dst = refs[which], o_ref.at[pl.ds(group, shards)]
        else:
            src, dst = refs[which].at[b], o_ref.at[group + (s ^ u)]
        copies.append(pltpu.make_async_copy(src, dst, sems.at[n]))
    for c in copies:
        c.start()
    for c in copies:
        c.wait()


def place(chunks, shards, shape, before):
    arrays, places = arrays_of(chunks)
    more = [] if before is None else [before]
    return pl.pallas_call(
        functools.partial(place_kernel, places, shards),
        in_specs=[whole()] * len(arrays) + [whole(pltpu.HBM)] * len(more),
        out_specs=whole(pltpu.HBM),
        out_shape=jax.ShapeDtypeStruct(shape, jnp.bfloat16),
        scratch_shapes=[pltpu.SemaphoreType.DMA((len(places),))],
        input_output_aliases={len(arrays): 0} if more else {},
        compiler_params=params(8),
        cost_estimate=cost(1000, 1000),
    )(*arrays, *more)


def shards(grads, momentum):
    count, rows, cols = grads.shape
    shard_count = lax.axis_size("shard")
    t = lax.axis_index("tensor")
    z2_plan, p31_plan, a0_plan = plans(shard_count)
    z2 = nesterov_group(grads, momentum, t ^ 2, shard_count)
    z2, grads, momentum = lax.optimization_barrier((z2, grads, momentum))
    p31 = nesterov(grads, momentum, p31_plan, shard_count)
    (a0,) = nesterov(grads, momentum, a0_plan, shard_count)
    chunks = exchange(z2, p31, a0, True)
    momentum_next, token = next_momentum(grads, momentum, chunks[0][0][0])
    before, part = early({k: chunks[k] for k in (0, 2)})
    x, g, z2 = first((0, 2), before, part, {k: chunks[k][0][0] for k in (1, 3)}, z2_plan, token)
    p31 = list(last(x, g, p31_plan, rows, cols))
    (a0,) = last(x, g, a0_plan, rows, cols)
    back = exchange(z2, p31, a0, False)
    update = place({k: back[k] for k in (0, 2)}, shard_count, grads.shape, None)
    update = place({k: back[k] for k in (1, 3)}, shard_count, grads.shape, update)
    return (momentum_next, update)


def solution(mesh):
    return jax.shard_map(
        shards,
        mesh=mesh,
        in_specs=(P(None, "shard", "tensor"), P(None, "shard", "tensor")),
        out_specs=(P(None, "shard", "tensor"), P(None, "shard", "tensor")),
        check_vma=False,
    )
```

```python
import functools

import jax
import jax.numpy as jnp
from jax import lax
from jax.experimental import pallas as pl
from jax.experimental.pallas import tpu as pltpu
from jax.sharding import PartitionSpec as P

MIB = 1024 * 1024


def whole(space=pltpu.VMEM):
    return pl.BlockSpec(memory_space=space)


def cost(flops, moved):
    return pl.CostEstimate(flops=flops, bytes_accessed=moved, transcendentals=0)


def params(mib):
    return pltpu.CompilerParams(vmem_limit_bytes=mib * MIB)


def nesterov_kernel(plan, shards, g_ref, m_ref, *outs):
    t, s = lax.axis_index("tensor"), lax.axis_index("shard")
    for out, pieces in zip(outs, plan):
        for i, (k, u) in enumerate(pieces):
            source = (t ^ k) * shards + (s ^ u)
            g = g_ref[source].astype(jnp.float32)
            m = 0.95 * m_ref[source] + g
            out[i] = (g + 0.95 * m).astype(jnp.bfloat16)


def nesterov(grads, momentum, plan, shards):
    count, rows, cols = grads.shape
    n = sum(len(pieces) for pieces in plan)
    return pl.pallas_call(
        functools.partial(nesterov_kernel, plan, shards),
        in_specs=[whole(), whole()],
        out_specs=[whole()] * len(plan),
        out_shape=[jax.ShapeDtypeStruct((len(pieces), rows, cols), jnp.bfloat16) for pieces in plan],
        compiler_params=params(8),
        cost_estimate=cost(6 * n * rows * cols, 8 * n * rows * cols),
    )(grads, momentum)


def momentum_kernel(g_ref, m_ref, after_ref, o_ref, token_ref):
    o_ref[...] = 0.95 * m_ref[...] + g_ref[...].astype(jnp.float32)
    token_ref[...] = jnp.zeros_like(token_ref)


def next_momentum(grads, momentum, after):
    count, rows, cols = grads.shape
    steps = 8
    spec = pl.BlockSpec((count // steps, rows, cols), lambda i: (i, 0, 0))
    return pl.pallas_call(
        momentum_kernel,
        grid=(steps,),
        in_specs=[spec, spec, whole(pl.ANY)],
        out_specs=[spec, whole()],
        out_shape=[
            jax.ShapeDtypeStruct(grads.shape, jnp.float32),
            jax.ShapeDtypeStruct((8, 128), jnp.float32),
        ],
        compiler_params=params(8),
        cost_estimate=cost(1000, 1000),
    )(grads, momentum, after)


def nesterov_group(grads, momentum, group, shards):
    g = lax.dynamic_slice_in_dim(grads, group * shards, shards, 0).astype(jnp.float32)
    m = lax.dynamic_slice_in_dim(momentum, group * shards, shards, 0)
    return (g + 0.95 * (0.95 * m + g)).astype(jnp.bfloat16)


def plans(shards):
    z2 = [(2, u) for u in range(shards)]
    p31 = [[(3, u), (1, u)] for u in range(shards)]
    a0 = [(0, u) for u in range(shards)]
    return [z2], p31, [a0]


def swap_tensor(piece, k):
    count = lax.axis_size("tensor")
    return lax.ppermute(piece, "tensor", [(t, t ^ k) for t in range(count)])


def swap_shard(piece, u):
    count = lax.axis_size("shard")
    return lax.ppermute(piece, "shard", [(s, s ^ u) for s in range(count)])


def regroup_kernel(plan, n, *refs):
    ins, outs = refs[:n], refs[n:]
    s = lax.axis_index("shard")
    for out, slabs in zip(outs, plan):
        for i, (a, b, moved, moves) in enumerate(slabs):
            out[i ^ s if moves else i] = ins[a][b ^ s if moved else b]


def regroup(arrays, plan):
    _, rows, cols = arrays[0].shape
    n = sum(len(slabs) for slabs in plan)
    return pl.pallas_call(
        functools.partial(regroup_kernel, plan, len(arrays)),
        in_specs=[whole()] * len(arrays),
        out_specs=[whole()] * len(plan),
        out_shape=[jax.ShapeDtypeStruct((len(slabs), rows, cols), jnp.bfloat16) for slabs in plan],
        compiler_params=params(8),
        cost_estimate=cost(0, 4 * n * rows * cols),
    )(*arrays)


def exchange(z2, p31, a0, moved):
    shards = len(p31)
    z2 = swap_tensor(z2, 2)
    p31 = [p31[0]] + [swap_shard(p31[u], u) for u in range(1, shards)]
    w3, w1 = regroup(p31, [[(u, i, False, not moved) for u in range(shards)] for i in range(2)])
    z3 = swap_tensor(w3, 3)
    z1 = swap_tensor(w1, 1)
    p20 = regroup((z2, a0), [[(0, u, moved, False), (1, u, False, False)] for u in range(shards)])
    p20 = [p20[0]] + [swap_shard(p20[u], u) for u in range(1, shards)]
    outs = {k: [(a, i) for a in p20] for i, k in enumerate((2, 0))}
    for k, a in ((3, z3), (1, z1)):
        outs[k] = [(a, u) for u in range(shards)] if moved else [(a, None)]
    return outs


def arrays_of(chunks):
    arrays, places = [], []
    for k in sorted(chunks):
        for u, (a, b) in enumerate(chunks[k]):
            known = [i for i, other in enumerate(arrays) if other is a]
            if not known:
                known = [len(arrays)]
                arrays.append(a)
            places.append((k, u, known[0], b))
    return arrays, places


def mm(a, b):
    return jnp.dot(a, b, preferred_element_type=jnp.float32)


def mm_rows(a, b):
    return lax.dot_general(a, b, (((1,), (1,)), ((), ())), preferred_element_type=jnp.float32)


def symmetric(x_ref, out_ref, finish=None, diagonal=0.0, mirror=True):
    order = x_ref.shape[0]
    tile = min(256, order)
    eye = lax.broadcasted_iota(jnp.int32, (tile, tile), 0) == lax.broadcasted_iota(jnp.int32, (tile, tile), 1)
    for i in range(order // tile):
        cols = slice(i * tile, (i + 1) * tile)
        below = slice(i * tile, order)
        part = mm_rows(x_ref[below, :], x_ref[cols, :])
        if finish is not None:
            part = finish(part, below, cols)
        if diagonal:
            top = part[:tile] + jnp.where(eye, diagonal, 0.0)
            out_ref[cols, cols] = top.astype(out_ref.dtype)
            if i + 1 == order // tile:
                break
            part = part[tile:].astype(out_ref.dtype)
            out_ref[(i + 1) * tile :, cols] = part
        else:
            part = part.astype(out_ref.dtype)
            out_ref[below, cols] = part
            part = part[tile:]
        if mirror and i + 1 < order // tile:
            out_ref[cols, (i + 1) * tile :] = part.T


def squares(x):
    x = x.astype(jnp.float32)
    return jnp.sum((x * x).reshape(x.shape[0] // 8, 8, x.shape[1]), axis=0)


def step_columns(gram_ref, x, power_ref):
    power = mm(gram_ref[...], x)
    power_ref[...] = power
    square = mm(gram_ref[...], power.astype(jnp.bfloat16))
    return 3.4445 * x.astype(jnp.float32) - 4.775 * power_ref[...] + 2.0315 * square


def finish(new, k, plan, outs):
    rows = outs[0].shape[1]
    gain = 0.2 * float(new.shape[0]) ** 0.5
    done = (gain * new.astype(jnp.float32)).astype(jnp.bfloat16)
    for out, pieces in zip(outs, plan):
        for i, (k_of, u) in enumerate(pieces):
            if k_of == k:
                out[i] = done[u * rows : (u + 1) * rows]


def early_kernel(places, n, *refs):
    ins, (x_ref, part_ref, sum_ref) = refs[:n], refs[n:]
    rows, cols = ins[0].shape[1:]
    at = {k: i * cols for i, k in enumerate(sorted({p[0] for p in places}))}
    for k, u, which, b in places:
        x_ref[u * rows : (u + 1) * rows, at[k] : at[k] + cols] = ins[which][b]
    sum_ref[...] = squares(x_ref[...])
    symmetric(x_ref, part_ref, mirror=False)


def early(chunks):
    arrays, places = arrays_of(chunks)
    _, rows, cols = arrays[0].shape
    order = rows * len(chunks[0])
    return pl.pallas_call(
        functools.partial(early_kernel, places, len(arrays)),
        in_specs=[whole()] * len(arrays),
        out_specs=[whole()] * 3,
        out_shape=[
            jax.ShapeDtypeStruct((order, cols * len(chunks)), jnp.bfloat16),
            jax.ShapeDtypeStruct((order, order), jnp.float32),
            jax.ShapeDtypeStruct((8, cols * len(chunks)), jnp.float32),
        ],
        compiler_params=params(16),
        cost_estimate=cost(1000, 1000),
    )(*arrays)


def first_kernel(early_ks, late_ks, plan, *refs):
    before_ref, part_ref, sum_ref, refs = refs[0], refs[1], refs[2], refs[3:]
    late_refs, (y_ref, h_ref), refs = refs[: len(late_ks)], refs[len(late_ks) + 1 :][:2], refs[len(late_ks) + 3 :]
    outs, (x_ref, g_ref, w_ref, power_ref) = refs[: len(plan)], refs[len(plan) :]
    order, cols = power_ref.shape
    where = {}
    for i, (k, ref) in enumerate(zip(late_ks, late_refs)):
        where[k] = (x_ref, slice(i * cols, (i + 1) * cols))
        x_ref[:, i * cols : (i + 1) * cols] = ref[...].reshape(order, cols)
    for i, k in enumerate(early_ks):
        where[k] = (before_ref, slice(i * cols, (i + 1) * cols))

    def chunk(k):
        ref, c = where[k]
        return ref[:, c]

    total = jnp.sum(sum_ref[...]) + jnp.sum(squares(x_ref[...]))
    scale = 1.0 / (jnp.sqrt(total) + 1e-07)

    def normalised(part, rows, cols):
        return (part + part_ref[rows, cols]) * (scale * scale)

    shift = 2.0

    def weights(square, rows, cols):
        return -4.775 * g_ref[rows, cols].astype(jnp.float32) + 2.0315 * square

    symmetric(x_ref, g_ref, finish=normalised)
    symmetric(g_ref, w_ref, finish=weights, diagonal=shift)
    for k in range(order // cols):
        c = slice(k * cols, (k + 1) * cols)
        x = (scale * chunk(k).astype(jnp.float32)).astype(jnp.bfloat16)
        y_ref[:, c] = ((3.4445 - shift) * x.astype(jnp.float32) + mm(w_ref[...], x)).astype(jnp.bfloat16)
    symmetric(y_ref, h_ref)
    for k in sorted({k for pieces in plan for k, _ in pieces}):
        new = step_columns(h_ref, y_ref[:, k * cols : (k + 1) * cols], power_ref)
        finish(new.astype(jnp.bfloat16), k, plan, outs)


def first(early_ks, before, part, sums, late, plan, after):
    shards, rows, cols = late[max(late)].shape
    order = shards * rows
    late_ks = sorted(late)
    square = jax.ShapeDtypeStruct((order, order), jnp.bfloat16)
    return pl.pallas_call(
        functools.partial(first_kernel, early_ks, late_ks, plan),
        in_specs=[whole()] * (3 + len(late)) + [whole(pl.ANY)],
        out_specs=[whole()] * (2 + len(plan)),
        out_shape=[square, square]
        + [jax.ShapeDtypeStruct((len(pieces), rows, cols), jnp.bfloat16) for pieces in plan],
        scratch_shapes=[pltpu.VMEM((order, len(late) * cols), jnp.bfloat16)]
        + [pltpu.VMEM((order, order), jnp.bfloat16)] * 2
        + [pltpu.VMEM((order, cols), jnp.float32)],
        compiler_params=params(20),
        cost_estimate=cost(7 * order**3, 12 * order**2),
    )(before, part, sums, *[late[k] for k in late_ks], after)


def last_kernel(plan, x_ref, g_ref, *refs):
    outs, power_ref = refs[:-1], refs[-1]
    order, cols = power_ref.shape
    for k in sorted({k for pieces in plan for k, _ in pieces}, reverse=True):
        new = step_columns(g_ref, x_ref[:, k * cols : (k + 1) * cols], power_ref)
        finish(new.astype(jnp.bfloat16), k, plan, outs)


def last(x, g, plan, rows, cols):
    order = x.shape[0]
    return pl.pallas_call(
        functools.partial(last_kernel, plan),
        in_specs=[whole()] * 2,
        out_specs=[whole()] * len(plan),
        out_shape=[jax.ShapeDtypeStruct((len(pieces), rows, cols), jnp.bfloat16) for pieces in plan],
        scratch_shapes=[pltpu.VMEM((order, cols), jnp.float32)],
        compiler_params=params(16),
        cost_estimate=cost(len(plan) // 8 * order**3 + order**3, 8 * order**2),
    )(x, g)


def place_kernel(places, shards, *refs):
    o_ref, sems = refs[-2:]
    t, s = lax.axis_index("tensor"), lax.axis_index("shard")
    copies = []
    for n, (k, u, which, b) in enumerate(places):
        group = (t ^ k) * shards
        if b is None:
            src, dst = refs[which], o_ref.at[pl.ds(group, shards)]
        else:
            src, dst = refs[which].at[b], o_ref.at[group + (s ^ u)]
        copies.append(pltpu.make_async_copy(src, dst, sems.at[n]))
    for c in copies:
        c.start()
    for c in copies:
        c.wait()


def place(chunks, shards, shape, before):
    arrays, places = arrays_of(chunks)
    more = [] if before is None else [before]
    return pl.pallas_call(
        functools.partial(place_kernel, places, shards),
        in_specs=[whole()] * len(arrays) + [whole(pltpu.HBM)] * len(more),
        out_specs=whole(pltpu.HBM),
        out_shape=jax.ShapeDtypeStruct(shape, jnp.bfloat16),
        scratch_shapes=[pltpu.SemaphoreType.DMA((len(places),))],
        input_output_aliases={len(arrays): 0} if more else {},
        compiler_params=params(8),
        cost_estimate=cost(1000, 1000),
    )(*arrays, *more)


def shards(grads, momentum):
    count, rows, cols = grads.shape
    shard_count = lax.axis_size("shard")
    t = lax.axis_index("tensor")
    z2_plan, p31_plan, a0_plan = plans(shard_count)
    z2 = nesterov_group(grads, momentum, t ^ 2, shard_count)
    z2, grads, momentum = lax.optimization_barrier((z2, grads, momentum))
    p31 = nesterov(grads, momentum, p31_plan, shard_count)
    (a0,) = nesterov(grads, momentum, a0_plan, shard_count)
    chunks = exchange(z2, p31, a0, True)
    momentum_next, token = next_momentum(grads, momentum, chunks[0][0][0])
    before, part, sums = early({k: chunks[k] for k in (0, 2)})
    x, g, z2 = first((0, 2), before, part, sums, {k: chunks[k][0][0] for k in (1, 3)}, z2_plan, token)
    p31 = list(last(x, g, p31_plan, rows, cols))
    (a0,) = last(x, g, a0_plan, rows, cols)
    back = exchange(z2, p31, a0, False)
    update = place({k: back[k] for k in (0, 2)}, shard_count, grads.shape, None)
    update = place({k: back[k] for k in (1, 3)}, shard_count, grads.shape, update)
    return (momentum_next, update)


def solution(mesh):
    return jax.shard_map(
        shards,
        mesh=mesh,
        in_specs=(P(None, "shard", "tensor"), P(None, "shard", "tensor")),
        out_specs=(P(None, "shard", "tensor"), P(None, "shard", "tensor")),
        check_vma=False,
    )
```

```python
import functools

import jax
import jax.numpy as jnp
from jax import lax
from jax.experimental import pallas as pl
from jax.experimental.pallas import tpu as pltpu
from jax.sharding import PartitionSpec as P

MIB = 1024 * 1024
FWD = (3, 2)
BACK = (2, 3)


def whole(space=pltpu.VMEM):
    return pl.BlockSpec(memory_space=space)


def cost(flops, moved):
    return pl.CostEstimate(flops=flops, bytes_accessed=moved, transcendentals=0)


def params(mib):
    return pltpu.CompilerParams(vmem_limit_bytes=mib * MIB)


def nesterov_kernel(plan, shards, g_ref, m_ref, *outs):
    t, s = lax.axis_index("tensor"), lax.axis_index("shard")
    for out, pieces in zip(outs, plan):
        for i, (k, u) in enumerate(pieces):
            source = (t ^ k) * shards + (s ^ u)
            g = g_ref[source].astype(jnp.float32)
            m = 0.95 * m_ref[source] + g
            out[i] = (g + 0.95 * m).astype(jnp.bfloat16)


def nesterov(grads, momentum, plan, shards):
    count, rows, cols = grads.shape
    n = sum(len(pieces) for pieces in plan)
    return pl.pallas_call(
        functools.partial(nesterov_kernel, plan, shards),
        in_specs=[whole(), whole()],
        out_specs=[whole()] * len(plan),
        out_shape=[jax.ShapeDtypeStruct((len(pieces), rows, cols), jnp.bfloat16) for pieces in plan],
        compiler_params=params(8),
        cost_estimate=cost(6 * n * rows * cols, 8 * n * rows * cols),
    )(grads, momentum)


def momentum_kernel(g_ref, m_ref, after_ref, o_ref, token_ref):
    o_ref[...] = 0.95 * m_ref[...] + g_ref[...].astype(jnp.float32)
    token_ref[...] = jnp.zeros_like(token_ref)


def next_momentum(grads, momentum, after):
    count, rows, cols = grads.shape
    steps = 8
    spec = pl.BlockSpec((count // steps, rows, cols), lambda i: (i, 0, 0))
    return pl.pallas_call(
        momentum_kernel,
        grid=(steps,),
        in_specs=[spec, spec, whole(pl.ANY)],
        out_specs=[spec, whole()],
        out_shape=[
            jax.ShapeDtypeStruct(grads.shape, jnp.float32),
            jax.ShapeDtypeStruct((8, 128), jnp.float32),
        ],
        compiler_params=params(8),
        cost_estimate=cost(1000, 1000),
    )(grads, momentum, after)


def nesterov_group(grads, momentum, group, shards):
    g = lax.dynamic_slice_in_dim(grads, group * shards, shards, 0).astype(jnp.float32)
    m = lax.dynamic_slice_in_dim(momentum, group * shards, shards, 0)
    return (g + 0.95 * (0.95 * m + g)).astype(jnp.bfloat16)


def plans(shards, early_k, late_k):
    early = [(early_k, u) for u in range(shards)]
    late = [[(late_k, u), (1, u)] for u in range(shards)]
    own = [(0, u) for u in range(shards)]
    return [early], late, [own]


def swap_tensor(piece, k):
    count = lax.axis_size("tensor")
    return lax.ppermute(piece, "tensor", [(t, t ^ k) for t in range(count)])


def swap_shard(piece, u):
    count = lax.axis_size("shard")
    return lax.ppermute(piece, "shard", [(s, s ^ u) for s in range(count)])


def regroup_kernel(plan, n, *refs):
    ins, outs = refs[:n], refs[n:]
    s = lax.axis_index("shard")
    for out, slabs in zip(outs, plan):
        for i, (a, b, moved, moves) in enumerate(slabs):
            out[i ^ s if moves else i] = ins[a][b ^ s if moved else b]


def regroup(arrays, plan):
    _, rows, cols = arrays[0].shape
    n = sum(len(slabs) for slabs in plan)
    return pl.pallas_call(
        functools.partial(regroup_kernel, plan, len(arrays)),
        in_specs=[whole()] * len(arrays),
        out_specs=[whole()] * len(plan),
        out_shape=[jax.ShapeDtypeStruct((len(slabs), rows, cols), jnp.bfloat16) for slabs in plan],
        compiler_params=params(8),
        cost_estimate=cost(0, 4 * n * rows * cols),
    )(*arrays)


def exchange(z2, p31, a0, moved, early_k, late_k):
    shards = len(p31)
    z2 = swap_tensor(z2, early_k)
    p31 = [p31[0]] + [swap_shard(p31[u], u) for u in range(1, shards)]
    w3, w1 = regroup(p31, [[(u, i, False, not moved) for u in range(shards)] for i in range(2)])
    z3 = swap_tensor(w3, late_k)
    z1 = swap_tensor(w1, 1)
    p20 = regroup((z2, a0), [[(0, u, moved, False), (1, u, False, False)] for u in range(shards)])
    p20 = [p20[0]] + [swap_shard(p20[u], u) for u in range(1, shards)]
    outs = {k: [(a, i) for a in p20] for i, k in enumerate((early_k, 0))}
    for k, a in ((late_k, z3), (1, z1)):
        outs[k] = [(a, u) for u in range(shards)] if moved else [(a, None)]
    return outs


def arrays_of(chunks):
    arrays, places = [], []
    for k in sorted(chunks):
        for u, (a, b) in enumerate(chunks[k]):
            known = [i for i, other in enumerate(arrays) if other is a]
            if not known:
                known = [len(arrays)]
                arrays.append(a)
            places.append((k, u, known[0], b))
    return arrays, places


def mm(a, b):
    return jnp.dot(a, b, preferred_element_type=jnp.float32)


def mm_rows(a, b):
    return lax.dot_general(a, b, (((1,), (1,)), ((), ())), preferred_element_type=jnp.float32)


def symmetric(x_ref, out_ref, finish=None, diagonal=0.0, mirror=True):
    order = x_ref.shape[0]
    tile = min(256, order)
    eye = lax.broadcasted_iota(jnp.int32, (tile, tile), 0) == lax.broadcasted_iota(jnp.int32, (tile, tile), 1)
    for i in range(order // tile):
        cols = slice(i * tile, (i + 1) * tile)
        below = slice(i * tile, order)
        part = mm_rows(x_ref[below, :], x_ref[cols, :])
        if finish is not None:
            part = finish(part, below, cols)
        if diagonal:
            top = part[:tile] + jnp.where(eye, diagonal, 0.0)
            out_ref[cols, cols] = top.astype(out_ref.dtype)
            if i + 1 == order // tile:
                break
            part = part[tile:].astype(out_ref.dtype)
            out_ref[(i + 1) * tile :, cols] = part
        else:
            part = part.astype(out_ref.dtype)
            out_ref[below, cols] = part
            part = part[tile:]
        if mirror and i + 1 < order // tile:
            out_ref[cols, (i + 1) * tile :] = part.T


def squares(x):
    x = x.astype(jnp.float32)
    return jnp.sum((x * x).reshape(x.shape[0] // 8, 8, x.shape[1]), axis=0)


def step_columns(gram_ref, x, power_ref):
    power = mm(gram_ref[...], x)
    power_ref[...] = power
    square = mm(gram_ref[...], power.astype(jnp.bfloat16))
    return 3.4445 * x.astype(jnp.float32) - 4.775 * power_ref[...] + 2.0315 * square


def finish(new, k, plan, outs):
    rows = outs[0].shape[1]
    gain = 0.2 * float(new.shape[0]) ** 0.5
    done = (gain * new.astype(jnp.float32)).astype(jnp.bfloat16)
    for out, pieces in zip(outs, plan):
        for i, (k_of, u) in enumerate(pieces):
            if k_of == k:
                out[i] = done[u * rows : (u + 1) * rows]


def early_kernel(places, n, *refs):
    ins, (x_ref, part_ref, sum_ref) = refs[:n], refs[n:]
    rows, cols = ins[0].shape[1:]
    at = {k: i * cols for i, k in enumerate(sorted({p[0] for p in places}))}
    for k, u, which, b in places:
        x_ref[u * rows : (u + 1) * rows, at[k] : at[k] + cols] = ins[which][b]
    sum_ref[...] = squares(x_ref[...])
    symmetric(x_ref, part_ref, mirror=False)


def early(chunks):
    arrays, places = arrays_of(chunks)
    _, rows, cols = arrays[0].shape
    order = rows * len(chunks[0])
    return pl.pallas_call(
        functools.partial(early_kernel, places, len(arrays)),
        in_specs=[whole()] * len(arrays),
        out_specs=[whole()] * 3,
        out_shape=[
            jax.ShapeDtypeStruct((order, cols * len(chunks)), jnp.bfloat16),
            jax.ShapeDtypeStruct((order, order), jnp.float32),
            jax.ShapeDtypeStruct((8, cols * len(chunks)), jnp.float32),
        ],
        compiler_params=params(16),
        cost_estimate=cost(1000, 1000),
    )(*arrays)


def first_kernel(early_ks, late_ks, plan, *refs):
    before_ref, part_ref, sum_ref, refs = refs[0], refs[1], refs[2], refs[3:]
    late_refs, (y_ref, h_ref), refs = refs[: len(late_ks)], refs[len(late_ks) + 1 :][:2], refs[len(late_ks) + 3 :]
    outs, (x_ref, g_ref, w_ref, power_ref) = refs[: len(plan)], refs[len(plan) :]
    order, cols = power_ref.shape
    where = {}
    for i, (k, ref) in enumerate(zip(late_ks, late_refs)):
        where[k] = (x_ref, slice(i * cols, (i + 1) * cols))
        x_ref[:, i * cols : (i + 1) * cols] = ref[...].reshape(order, cols)
    for i, k in enumerate(early_ks):
        where[k] = (before_ref, slice(i * cols, (i + 1) * cols))

    def chunk(k):
        ref, c = where[k]
        return ref[:, c]

    total = jnp.sum(sum_ref[...]) + jnp.sum(squares(x_ref[...]))
    scale = 1.0 / (jnp.sqrt(total) + 1e-07)

    def normalised(part, rows, cols):
        return (part + part_ref[rows, cols]) * (scale * scale)

    shift = 2.0

    def weights(square, rows, cols):
        return -4.775 * g_ref[rows, cols].astype(jnp.float32) + 2.0315 * square

    symmetric(x_ref, g_ref, finish=normalised)
    symmetric(g_ref, w_ref, finish=weights, diagonal=shift)
    for k in range(order // cols):
        c = slice(k * cols, (k + 1) * cols)
        x = (scale * chunk(k).astype(jnp.float32)).astype(jnp.bfloat16)
        y_ref[:, c] = ((3.4445 - shift) * x.astype(jnp.float32) + mm(w_ref[...], x)).astype(jnp.bfloat16)
    symmetric(y_ref, h_ref)
    for k in sorted({k for pieces in plan for k, _ in pieces}):
        new = step_columns(h_ref, y_ref[:, k * cols : (k + 1) * cols], power_ref)
        finish(new.astype(jnp.bfloat16), k, plan, outs)


def first(early_ks, before, part, sums, late, plan, after):
    shards, rows, cols = late[max(late)].shape
    order = shards * rows
    late_ks = sorted(late)
    square = jax.ShapeDtypeStruct((order, order), jnp.bfloat16)
    return pl.pallas_call(
        functools.partial(first_kernel, early_ks, late_ks, plan),
        in_specs=[whole()] * (3 + len(late)) + [whole(pl.ANY)],
        out_specs=[whole()] * (2 + len(plan)),
        out_shape=[square, square]
        + [jax.ShapeDtypeStruct((len(pieces), rows, cols), jnp.bfloat16) for pieces in plan],
        scratch_shapes=[pltpu.VMEM((order, len(late) * cols), jnp.bfloat16)]
        + [pltpu.VMEM((order, order), jnp.bfloat16)] * 2
        + [pltpu.VMEM((order, cols), jnp.float32)],
        compiler_params=params(20),
        cost_estimate=cost(7 * order**3, 12 * order**2),
    )(before, part, sums, *[late[k] for k in late_ks], after)


def last_kernel(plan, x_ref, g_ref, *refs):
    outs, power_ref = refs[:-1], refs[-1]
    order, cols = power_ref.shape
    for k in sorted({k for pieces in plan for k, _ in pieces}, reverse=True):
        new = step_columns(g_ref, x_ref[:, k * cols : (k + 1) * cols], power_ref)
        finish(new.astype(jnp.bfloat16), k, plan, outs)


def last(x, g, plan, rows, cols):
    order = x.shape[0]
    return pl.pallas_call(
        functools.partial(last_kernel, plan),
        in_specs=[whole()] * 2,
        out_specs=[whole()] * len(plan),
        out_shape=[jax.ShapeDtypeStruct((len(pieces), rows, cols), jnp.bfloat16) for pieces in plan],
        scratch_shapes=[pltpu.VMEM((order, cols), jnp.float32)],
        compiler_params=params(16),
        cost_estimate=cost(len(plan) // 8 * order**3 + order**3, 8 * order**2),
    )(x, g)


def place_kernel(places, shards, *refs):
    o_ref, sems = refs[-2:]
    t, s = lax.axis_index("tensor"), lax.axis_index("shard")
    copies = []
    for n, (k, u, which, b) in enumerate(places):
        group = (t ^ k) * shards
        if b is None:
            src, dst = refs[which], o_ref.at[pl.ds(group, shards)]
        else:
            src, dst = refs[which].at[b], o_ref.at[group + (s ^ u)]
        copies.append(pltpu.make_async_copy(src, dst, sems.at[n]))
    for c in copies:
        c.start()
    for c in copies:
        c.wait()


def place(chunks, shards, shape, before):
    arrays, places = arrays_of(chunks)
    more = [] if before is None else [before]
    return pl.pallas_call(
        functools.partial(place_kernel, places, shards),
        in_specs=[whole()] * len(arrays) + [whole(pltpu.HBM)] * len(more),
        out_specs=whole(pltpu.HBM),
        out_shape=jax.ShapeDtypeStruct(shape, jnp.bfloat16),
        scratch_shapes=[pltpu.SemaphoreType.DMA((len(places),))],
        input_output_aliases={len(arrays): 0} if more else {},
        compiler_params=params(8),
        cost_estimate=cost(1000, 1000),
    )(*arrays, *more)


def shards(grads, momentum):
    count, rows, cols = grads.shape
    shard_count = lax.axis_size("shard")
    t = lax.axis_index("tensor")
    ks = early_k, late_k = FWD
    _, p31_plan, a0_plan = plans(shard_count, *ks)
    z2 = nesterov_group(grads, momentum, t ^ early_k, shard_count)
    z2, grads, momentum = lax.optimization_barrier((z2, grads, momentum))
    p31 = nesterov(grads, momentum, p31_plan, shard_count)
    (a0,) = nesterov(grads, momentum, a0_plan, shard_count)
    chunks = exchange(z2, p31, a0, True, *ks)
    momentum_next, token = next_momentum(grads, momentum, chunks[0][0][0])
    before, part, sums = early({k: chunks[k] for k in (0, early_k)})
    late = {k: chunks[k][0][0] for k in (1, late_k)}
    fk = early_k

    ks = early_k, late_k = BACK
    z2_plan, p31_plan, a0_plan = plans(shard_count, *ks)
    x, g, z2 = first((0, fk), before, part, sums, late, z2_plan, token)
    p31 = list(last(x, g, p31_plan, rows, cols))
    (a0,) = last(x, g, a0_plan, rows, cols)
    back = exchange(z2, p31, a0, False, *ks)
    update = place({k: back[k] for k in (0, early_k)}, shard_count, grads.shape, None)
    update = place({k: back[k] for k in (1, late_k)}, shard_count, grads.shape, update)
    return (momentum_next, update)


def solution(mesh):
    return jax.shard_map(
        shards,
        mesh=mesh,
        in_specs=(P(None, "shard", "tensor"), P(None, "shard", "tensor")),
        out_specs=(P(None, "shard", "tensor"), P(None, "shard", "tensor")),
        check_vma=False,
    )
```

```python
import functools

import jax
import jax.numpy as jnp
from jax import lax
from jax.experimental import pallas as pl
from jax.experimental.pallas import tpu as pltpu
from jax.sharding import PartitionSpec as P

MIB = 1024 * 1024
FWD = (3, 2)
BACK = (2, 3)


def whole(space=pltpu.VMEM):
    return pl.BlockSpec(memory_space=space)


def cost(flops, moved):
    return pl.CostEstimate(flops=flops, bytes_accessed=moved, transcendentals=0)


def params(mib):
    return pltpu.CompilerParams(vmem_limit_bytes=mib * MIB)


def nesterov_kernel(plan, shards, g_ref, m_ref, *outs):
    t, s = lax.axis_index("tensor"), lax.axis_index("shard")
    for out, pieces in zip(outs, plan):
        for i, (k, u) in enumerate(pieces):
            source = (t ^ k) * shards + (s ^ u)
            g = g_ref[source].astype(jnp.float32)
            m = 0.95 * m_ref[source] + g
            out[i] = (g + 0.95 * m).astype(jnp.bfloat16)


def nesterov(grads, momentum, plan, shards):
    count, rows, cols = grads.shape
    n = sum(len(pieces) for pieces in plan)
    return pl.pallas_call(
        functools.partial(nesterov_kernel, plan, shards),
        in_specs=[whole(), whole()],
        out_specs=[whole()] * len(plan),
        out_shape=[jax.ShapeDtypeStruct((len(pieces), rows, cols), jnp.bfloat16) for pieces in plan],
        compiler_params=params(8),
        cost_estimate=cost(6 * n * rows * cols, 8 * n * rows * cols),
    )(grads, momentum)


def momentum_kernel(g_ref, m_ref, after_ref, o_ref, token_ref):
    o_ref[...] = 0.95 * m_ref[...] + g_ref[...].astype(jnp.float32)
    token_ref[...] = jnp.zeros_like(token_ref)


def next_momentum(grads, momentum, after):
    count, rows, cols = grads.shape
    steps = 8
    spec = pl.BlockSpec((count // steps, rows, cols), lambda i: (i, 0, 0))
    return pl.pallas_call(
        momentum_kernel,
        grid=(steps,),
        in_specs=[spec, spec, whole(pl.ANY)],
        out_specs=[spec, whole()],
        out_shape=[
            jax.ShapeDtypeStruct(grads.shape, jnp.float32),
            jax.ShapeDtypeStruct((8, 128), jnp.float32),
        ],
        compiler_params=params(8),
        cost_estimate=cost(1000, 1000),
    )(grads, momentum, after)


def nesterov_group(grads, momentum, group, shards):
    g = lax.dynamic_slice_in_dim(grads, group * shards, shards, 0, allow_negative_indices=False).astype(jnp.float32)
    m = lax.dynamic_slice_in_dim(momentum, group * shards, shards, 0, allow_negative_indices=False)
    return (g + 0.95 * (0.95 * m + g)).astype(jnp.bfloat16)


def plans(shards, early_k, late_k):
    early = [(early_k, u) for u in range(shards)]
    late = [[(late_k, u), (1, u)] for u in range(shards)]
    own = [(0, u) for u in range(shards)]
    return [early], late, [own]


def swap_tensor(piece, k):
    count = lax.axis_size("tensor")
    return lax.ppermute(piece, "tensor", [(t, t ^ k) for t in range(count)])


def swap_shard(piece, u):
    count = lax.axis_size("shard")
    return lax.ppermute(piece, "shard", [(s, s ^ u) for s in range(count)])


def regroup_kernel(plan, n, *refs):
    ins, outs = refs[:n], refs[n:]
    s = lax.axis_index("shard")
    for out, slabs in zip(outs, plan):
        for i, (a, b, moved, moves) in enumerate(slabs):
            out[i ^ s if moves else i] = ins[a][b ^ s if moved else b]


def regroup(arrays, plan):
    _, rows, cols = arrays[0].shape
    n = sum(len(slabs) for slabs in plan)
    return pl.pallas_call(
        functools.partial(regroup_kernel, plan, len(arrays)),
        in_specs=[whole()] * len(arrays),
        out_specs=[whole()] * len(plan),
        out_shape=[jax.ShapeDtypeStruct((len(slabs), rows, cols), jnp.bfloat16) for slabs in plan],
        compiler_params=params(8),
        cost_estimate=cost(0, 4 * n * rows * cols),
    )(*arrays)


def exchange(z2, p31, a0, moved, early_k, late_k):
    shards = len(p31)
    z2 = swap_tensor(z2, early_k)
    p31 = [p31[0]] + [swap_shard(p31[u], u) for u in range(1, shards)]
    w3, w1 = regroup(p31, [[(u, i, False, not moved) for u in range(shards)] for i in range(2)])
    z3 = swap_tensor(w3, late_k)
    z1 = swap_tensor(w1, 1)
    p20 = regroup((z2, a0), [[(0, u, moved, False), (1, u, False, False)] for u in range(shards)])
    p20 = [p20[0]] + [swap_shard(p20[u], u) for u in range(1, shards)]
    outs = {k: [(a, i) for a in p20] for i, k in enumerate((early_k, 0))}
    for k, a in ((late_k, z3), (1, z1)):
        outs[k] = [(a, u) for u in range(shards)] if moved else [(a, None)]
    return outs


def arrays_of(chunks):
    arrays, places = [], []
    for k in sorted(chunks):
        for u, (a, b) in enumerate(chunks[k]):
            known = [i for i, other in enumerate(arrays) if other is a]
            if not known:
                known = [len(arrays)]
                arrays.append(a)
            places.append((k, u, known[0], b))
    return arrays, places


def mm(a, b):
    return jnp.dot(a, b, preferred_element_type=jnp.float32)


def mm_rows(a, b):
    return lax.dot_general(a, b, (((1,), (1,)), ((), ())), preferred_element_type=jnp.float32)


def symmetric(x_ref, out_ref, finish=None, diagonal=0.0, mirror=True):
    order = x_ref.shape[0]
    tile = min(256, order)
    eye = lax.broadcasted_iota(jnp.int32, (tile, tile), 0) == lax.broadcasted_iota(jnp.int32, (tile, tile), 1)
    for i in range(order // tile):
        cols = slice(i * tile, (i + 1) * tile)
        below = slice(i * tile, order)
        part = mm_rows(x_ref[below, :], x_ref[cols, :])
        if finish is not None:
            part = finish(part, below, cols)
        if diagonal:
            top = part[:tile] + jnp.where(eye, diagonal, 0.0)
            out_ref[cols, cols] = top.astype(out_ref.dtype)
            if i + 1 == order // tile:
                break
            part = part[tile:].astype(out_ref.dtype)
            out_ref[(i + 1) * tile :, cols] = part
        else:
            part = part.astype(out_ref.dtype)
            out_ref[below, cols] = part
            part = part[tile:]
        if mirror and i + 1 < order // tile:
            out_ref[cols, (i + 1) * tile :] = part.T


def squares(x):
    x = x.astype(jnp.float32)
    return jnp.sum((x * x).reshape(x.shape[0] // 8, 8, x.shape[1]), axis=0)


def step_columns(gram_ref, x, power_ref):
    power = mm(gram_ref[...], x)
    power_ref[...] = power
    square = mm(gram_ref[...], power.astype(jnp.bfloat16))
    return 3.4445 * x.astype(jnp.float32) - 4.775 * power_ref[...] + 2.0315 * square


def finish(new, k, plan, outs):
    rows = outs[0].shape[1]
    gain = 0.2 * float(new.shape[0]) ** 0.5
    done = (gain * new.astype(jnp.float32)).astype(jnp.bfloat16)
    for out, pieces in zip(outs, plan):
        for i, (k_of, u) in enumerate(pieces):
            if k_of == k:
                out[i] = done[u * rows : (u + 1) * rows]


def early_kernel(places, n, *refs):
    ins, (x_ref, part_ref, sum_ref) = refs[:n], refs[n:]
    rows, cols = ins[0].shape[1:]
    at = {k: i * cols for i, k in enumerate(sorted({p[0] for p in places}))}
    for k, u, which, b in places:
        x_ref[u * rows : (u + 1) * rows, at[k] : at[k] + cols] = ins[which][b]
    sum_ref[...] = squares(x_ref[...])
    symmetric(x_ref, part_ref, mirror=False)


def early(chunks):
    arrays, places = arrays_of(chunks)
    _, rows, cols = arrays[0].shape
    order = rows * len(chunks[0])
    return pl.pallas_call(
        functools.partial(early_kernel, places, len(arrays)),
        in_specs=[whole()] * len(arrays),
        out_specs=[whole()] * 3,
        out_shape=[
            jax.ShapeDtypeStruct((order, cols * len(chunks)), jnp.bfloat16),
            jax.ShapeDtypeStruct((order, order), jnp.float32),
            jax.ShapeDtypeStruct((8, cols * len(chunks)), jnp.float32),
        ],
        compiler_params=params(16),
        cost_estimate=cost(1000, 1000),
    )(*arrays)


def first_kernel(early_ks, late_ks, plan, *refs):
    before_ref, part_ref, sum_ref, refs = refs[0], refs[1], refs[2], refs[3:]
    late_refs, (y_ref, h_ref), refs = refs[: len(late_ks)], refs[len(late_ks) + 1 :][:2], refs[len(late_ks) + 3 :]
    outs, (x_ref, g_ref, w_ref, power_ref) = refs[: len(plan)], refs[len(plan) :]
    order, cols = power_ref.shape
    where = {}
    for i, (k, ref) in enumerate(zip(late_ks, late_refs)):
        where[k] = (x_ref, slice(i * cols, (i + 1) * cols))
        x_ref[:, i * cols : (i + 1) * cols] = ref[...].reshape(order, cols)
    for i, k in enumerate(early_ks):
        where[k] = (before_ref, slice(i * cols, (i + 1) * cols))

    def chunk(k):
        ref, c = where[k]
        return ref[:, c]

    total = jnp.sum(sum_ref[...]) + jnp.sum(squares(x_ref[...]))
    scale = 1.0 / (jnp.sqrt(total) + 1e-07)

    def normalised(part, rows, cols):
        return (part + part_ref[rows, cols]) * (scale * scale)

    shift = 2.0

    def weights(square, rows, cols):
        return -4.775 * g_ref[rows, cols].astype(jnp.float32) + 2.0315 * square

    symmetric(x_ref, g_ref, finish=normalised)
    symmetric(g_ref, w_ref, finish=weights, diagonal=shift)
    for ref, ks in ((before_ref, early_ks), (x_ref, late_ks)):
        x = (scale * ref[...].astype(jnp.float32)).astype(jnp.bfloat16)
        new = ((3.4445 - shift) * x.astype(jnp.float32) + mm(w_ref[...], x)).astype(jnp.bfloat16)
        for i, k in enumerate(ks):
            y_ref[:, k * cols : (k + 1) * cols] = new[:, i * cols : (i + 1) * cols]
    symmetric(y_ref, h_ref)
    for k in sorted({k for pieces in plan for k, _ in pieces}):
        new = step_columns(h_ref, y_ref[:, k * cols : (k + 1) * cols], power_ref)
        finish(new.astype(jnp.bfloat16), k, plan, outs)


def first(early_ks, before, part, sums, late, plan, after):
    shards, rows, cols = late[max(late)].shape
    order = shards * rows
    late_ks = sorted(late)
    square = jax.ShapeDtypeStruct((order, order), jnp.bfloat16)
    return pl.pallas_call(
        functools.partial(first_kernel, early_ks, late_ks, plan),
        in_specs=[whole()] * (3 + len(late)) + [whole(pl.ANY)],
        out_specs=[whole()] * (2 + len(plan)),
        out_shape=[square, square]
        + [jax.ShapeDtypeStruct((len(pieces), rows, cols), jnp.bfloat16) for pieces in plan],
        scratch_shapes=[pltpu.VMEM((order, len(late) * cols), jnp.bfloat16)]
        + [pltpu.VMEM((order, order), jnp.bfloat16)] * 2
        + [pltpu.VMEM((order, cols), jnp.float32)],
        compiler_params=params(20),
        cost_estimate=cost(7 * order**3, 12 * order**2),
    )(before, part, sums, *[late[k] for k in late_ks], after)


def last_kernel(plan, x_ref, g_ref, *refs):
    outs, power_ref = refs[:-1], refs[-1]
    order, cols = power_ref.shape
    for k in sorted({k for pieces in plan for k, _ in pieces}, reverse=True):
        new = step_columns(g_ref, x_ref[:, k * cols : (k + 1) * cols], power_ref)
        finish(new.astype(jnp.bfloat16), k, plan, outs)


def last(x, g, plan, rows, cols):
    order = x.shape[0]
    return pl.pallas_call(
        functools.partial(last_kernel, plan),
        in_specs=[whole()] * 2,
        out_specs=[whole()] * len(plan),
        out_shape=[jax.ShapeDtypeStruct((len(pieces), rows, cols), jnp.bfloat16) for pieces in plan],
        scratch_shapes=[pltpu.VMEM((order, cols), jnp.float32)],
        compiler_params=params(16),
        cost_estimate=cost(len(plan) // 8 * order**3 + order**3, 8 * order**2),
    )(x, g)


def place_kernel(places, shards, *refs):
    o_ref, sems = refs[-2:]
    t, s = lax.axis_index("tensor"), lax.axis_index("shard")
    copies = []
    for n, (k, u, which, b) in enumerate(places):
        group = (t ^ k) * shards
        if b is None:
            src, dst = refs[which], o_ref.at[pl.ds(group, shards)]
        else:
            src, dst = refs[which].at[b], o_ref.at[group + (s ^ u)]
        copies.append(pltpu.make_async_copy(src, dst, sems.at[n]))
    for c in copies:
        c.start()
    for c in copies:
        c.wait()


def place(chunks, shards, shape, before):
    arrays, places = arrays_of(chunks)
    more = [] if before is None else [before]
    return pl.pallas_call(
        functools.partial(place_kernel, places, shards),
        in_specs=[whole()] * len(arrays) + [whole(pltpu.HBM)] * len(more),
        out_specs=whole(pltpu.HBM),
        out_shape=jax.ShapeDtypeStruct(shape, jnp.bfloat16),
        scratch_shapes=[pltpu.SemaphoreType.DMA((len(places),))],
        input_output_aliases={len(arrays): 0} if more else {},
        compiler_params=params(8),
        cost_estimate=cost(1000, 1000),
    )(*arrays, *more)


def shards(grads, momentum):
    count, rows, cols = grads.shape
    shard_count = lax.axis_size("shard")
    t = lax.axis_index("tensor")
    ks = early_k, late_k = FWD
    _, p31_plan, a0_plan = plans(shard_count, *ks)
    z2 = nesterov_group(grads, momentum, t ^ early_k, shard_count)
    z2, grads, momentum = lax.optimization_barrier((z2, grads, momentum))
    p31 = nesterov(grads, momentum, p31_plan, shard_count)
    (a0,) = nesterov(grads, momentum, a0_plan, shard_count)
    chunks = exchange(z2, p31, a0, True, *ks)
    momentum_next, token = next_momentum(grads, momentum, chunks[0][0][0])
    before, part, sums = early({k: chunks[k] for k in (0, early_k)})
    late = {k: chunks[k][0][0] for k in (1, late_k)}
    fk = early_k

    ks = early_k, late_k = BACK
    z2_plan, p31_plan, a0_plan = plans(shard_count, *ks)
    x, g, z2 = first((0, fk), before, part, sums, late, z2_plan, token)
    p31 = list(last(x, g, p31_plan, rows, cols))
    (a0,) = last(x, g, a0_plan, rows, cols)
    back = exchange(z2, p31, a0, False, *ks)
    update = place({k: back[k] for k in (0, early_k)}, shard_count, grads.shape, None)
    update = place({k: back[k] for k in (1, late_k)}, shard_count, grads.shape, update)
    return (momentum_next, update)


def solution(mesh):
    return jax.shard_map(
        shards,
        mesh=mesh,
        in_specs=(P(None, "shard", "tensor"), P(None, "shard", "tensor")),
        out_specs=(P(None, "shard", "tensor"), P(None, "shard", "tensor")),
        check_vma=False,
    )
```

```python
import functools

import jax
import jax.numpy as jnp
from jax import lax
from jax.experimental import pallas as pl
from jax.experimental.pallas import tpu as pltpu
from jax.sharding import PartitionSpec as P

MIB = 1024 * 1024
FWD = (3, 2)
BACK = (2, 3)


def whole(space=pltpu.VMEM):
    return pl.BlockSpec(memory_space=space)


def cost(flops, moved):
    return pl.CostEstimate(flops=flops, bytes_accessed=moved, transcendentals=0)


def params(mib):
    return pltpu.CompilerParams(vmem_limit_bytes=mib * MIB)


def nesterov_kernel(plan, shards, g_ref, m_ref, *outs):
    t, s = lax.axis_index("tensor"), lax.axis_index("shard")
    for out, pieces in zip(outs, plan):
        for i, (k, u) in enumerate(pieces):
            source = (t ^ k) * shards + (s ^ u)
            g = g_ref[source].astype(jnp.float32)
            m = 0.95 * m_ref[source] + g
            out[i] = (g + 0.95 * m).astype(jnp.bfloat16)


def nesterov(grads, momentum, plan, shards):
    count, rows, cols = grads.shape
    n = sum(len(pieces) for pieces in plan)
    return pl.pallas_call(
        functools.partial(nesterov_kernel, plan, shards),
        in_specs=[whole(), whole()],
        out_specs=[whole()] * len(plan),
        out_shape=[jax.ShapeDtypeStruct((len(pieces), rows, cols), jnp.bfloat16) for pieces in plan],
        compiler_params=params(8),
        cost_estimate=cost(6 * n * rows * cols, 8 * n * rows * cols),
    )(grads, momentum)


def momentum_kernel(g_ref, m_ref, after_ref, o_ref, token_ref):
    o_ref[...] = 0.95 * m_ref[...] + g_ref[...].astype(jnp.float32)
    token_ref[...] = jnp.zeros_like(token_ref)


def next_momentum(grads, momentum, after):
    count, rows, cols = grads.shape
    steps = 8
    spec = pl.BlockSpec((count // steps, rows, cols), lambda i: (i, 0, 0))
    return pl.pallas_call(
        momentum_kernel,
        grid=(steps,),
        in_specs=[spec, spec, whole(pl.ANY)],
        out_specs=[spec, whole()],
        out_shape=[
            jax.ShapeDtypeStruct(grads.shape, jnp.float32),
            jax.ShapeDtypeStruct((8, 128), jnp.float32),
        ],
        compiler_params=params(8),
        cost_estimate=cost(1000, 1000),
    )(grads, momentum, after)


def nesterov_group(grads, momentum, group, shards):
    g = lax.dynamic_slice_in_dim(grads, group * shards, shards, 0, allow_negative_indices=False).astype(jnp.float32)
    m = lax.dynamic_slice_in_dim(momentum, group * shards, shards, 0, allow_negative_indices=False)
    return (g + 0.95 * (0.95 * m + g)).astype(jnp.bfloat16)


def plans(shards, early_k, late_k):
    early = [(early_k, u) for u in range(shards)]
    late = [[(late_k, u), (1, u)] for u in range(shards)]
    own = [(0, u) for u in range(shards)]
    return [early], late, [own]


def swap_tensor(piece, k):
    count = lax.axis_size("tensor")
    return lax.ppermute(piece, "tensor", [(t, t ^ k) for t in range(count)])


def swap_shard(piece, u):
    count = lax.axis_size("shard")
    return lax.ppermute(piece, "shard", [(s, s ^ u) for s in range(count)])


def regroup_kernel(plan, n, *refs):
    ins, outs = refs[:n], refs[n:]
    s = lax.axis_index("shard")
    for out, slabs in zip(outs, plan):
        for i, (a, b, moved, moves) in enumerate(slabs):
            out[i ^ s if moves else i] = ins[a][b ^ s if moved else b]


def regroup(arrays, plan):
    _, rows, cols = arrays[0].shape
    n = sum(len(slabs) for slabs in plan)
    return pl.pallas_call(
        functools.partial(regroup_kernel, plan, len(arrays)),
        in_specs=[whole()] * len(arrays),
        out_specs=[whole()] * len(plan),
        out_shape=[jax.ShapeDtypeStruct((len(slabs), rows, cols), jnp.bfloat16) for slabs in plan],
        compiler_params=params(8),
        cost_estimate=cost(0, 4 * n * rows * cols),
    )(*arrays)


def exchange(z2, p31, a0, moved, early_k, late_k):
    shards = len(p31)
    z2 = swap_tensor(z2, early_k)
    p31 = [p31[0]] + [swap_shard(p31[u], u) for u in range(1, shards)]
    w3, w1 = regroup(p31, [[(u, i, False, not moved) for u in range(shards)] for i in range(2)])
    z3 = swap_tensor(w3, late_k)
    z1 = swap_tensor(w1, 1)
    p20 = regroup((z2, a0), [[(0, u, moved, False), (1, u, False, False)] for u in range(shards)])
    p20 = [p20[0]] + [swap_shard(p20[u], u) for u in range(1, shards)]
    outs = {k: [(a, i) for a in p20] for i, k in enumerate((early_k, 0))}
    for k, a in ((late_k, z3), (1, z1)):
        outs[k] = [(a, u) for u in range(shards)] if moved else [(a, None)]
    return outs


def arrays_of(chunks):
    arrays, places = [], []
    for k in sorted(chunks):
        for u, (a, b) in enumerate(chunks[k]):
            known = [i for i, other in enumerate(arrays) if other is a]
            if not known:
                known = [len(arrays)]
                arrays.append(a)
            places.append((k, u, known[0], b))
    return arrays, places


def mm(a, b):
    return jnp.dot(a, b, preferred_element_type=jnp.float32)


def mm_rows(a, b):
    return lax.dot_general(a, b, (((1,), (1,)), ((), ())), preferred_element_type=jnp.float32)


def symmetric(x_ref, out_ref, finish=None, diagonal=0.0, mirror=True):
    order = x_ref.shape[0]
    tile = min(256, order)
    eye = lax.broadcasted_iota(jnp.int32, (tile, tile), 0) == lax.broadcasted_iota(jnp.int32, (tile, tile), 1)
    for i in range(order // tile):
        cols = slice(i * tile, (i + 1) * tile)
        below = slice(i * tile, order)
        part = mm_rows(x_ref[below, :], x_ref[cols, :])
        if finish is not None:
            part = finish(part, below, cols)
        if diagonal:
            top = part[:tile] + jnp.where(eye, diagonal, 0.0)
            out_ref[cols, cols] = top.astype(out_ref.dtype)
            if i + 1 == order // tile:
                break
            part = part[tile:].astype(out_ref.dtype)
            out_ref[(i + 1) * tile :, cols] = part
        else:
            part = part.astype(out_ref.dtype)
            out_ref[below, cols] = part
            part = part[tile:]
        if mirror and i + 1 < order // tile:
            out_ref[cols, (i + 1) * tile :] = part.T


def squares(x):
    x = x.astype(jnp.float32)
    return jnp.sum((x * x).reshape(x.shape[0] // 8, 8, x.shape[1]), axis=0)


def step_columns(gram_ref, x, power_ref):
    power = mm(gram_ref[...], x)
    power_ref[...] = power
    square = mm(gram_ref[...], power.astype(jnp.bfloat16))
    return 3.4445 * x.astype(jnp.float32) - 4.775 * power_ref[...] + 2.0315 * square


def finish(new, k, plan, outs):
    rows = outs[0].shape[1]
    gain = 0.2 * float(new.shape[0]) ** 0.5
    done = (gain * new.astype(jnp.float32)).astype(jnp.bfloat16)
    for out, pieces in zip(outs, plan):
        for i, (k_of, u) in enumerate(pieces):
            if k_of == k:
                out[i] = done[u * rows : (u + 1) * rows]


def early_kernel(places, n, *refs):
    ins, (x_ref, part_ref, sum_ref) = refs[:n], refs[n:]
    rows, cols = ins[0].shape[1:]
    at = {k: i * cols for i, k in enumerate(sorted({p[0] for p in places}))}
    for k, u, which, b in places:
        x_ref[u * rows : (u + 1) * rows, at[k] : at[k] + cols] = ins[which][b]
    sum_ref[...] = squares(x_ref[...])
    symmetric(x_ref, part_ref, mirror=False)


def early(chunks):
    arrays, places = arrays_of(chunks)
    _, rows, cols = arrays[0].shape
    order = rows * len(chunks[0])
    return pl.pallas_call(
        functools.partial(early_kernel, places, len(arrays)),
        in_specs=[whole()] * len(arrays),
        out_specs=[whole()] * 3,
        out_shape=[
            jax.ShapeDtypeStruct((order, cols * len(chunks)), jnp.bfloat16),
            jax.ShapeDtypeStruct((order, order), jnp.float32),
            jax.ShapeDtypeStruct((8, cols * len(chunks)), jnp.float32),
        ],
        compiler_params=params(16),
        cost_estimate=cost(1000, 1000),
    )(*arrays)


def first_kernel(early_ks, late_ks, plan, *refs):
    before_ref, part_ref, sum_ref, refs = refs[0], refs[1], refs[2], refs[3:]
    late_refs, (y_ref, h_ref), refs = refs[: len(late_ks)], refs[len(late_ks) + 1 :][:2], refs[len(late_ks) + 3 :]
    outs, (x_ref, g_ref, w_ref, power_ref) = refs[: len(plan)], refs[len(plan) :]
    order, cols = power_ref.shape
    where = {}
    for i, (k, ref) in enumerate(zip(late_ks, late_refs)):
        where[k] = (x_ref, slice(i * cols, (i + 1) * cols))
        x_ref[:, i * cols : (i + 1) * cols] = ref[...].reshape(order, cols)
    for i, k in enumerate(early_ks):
        where[k] = (before_ref, slice(i * cols, (i + 1) * cols))

    def chunk(k):
        ref, c = where[k]
        return ref[:, c]

    total = jnp.sum(sum_ref[...]) + jnp.sum(squares(x_ref[...]))
    scale = 1.0 / (jnp.sqrt(total) + 1e-07)

    def normalised(part, rows, cols):
        return (part + part_ref[rows, cols]) * (scale * scale)

    shift = 2.0

    def weights(square, rows, cols):
        return -4.775 * g_ref[rows, cols].astype(jnp.float32) + 2.0315 * square

    symmetric(x_ref, g_ref, finish=normalised)
    symmetric(g_ref, w_ref, finish=weights, diagonal=shift)
    for ref, ks in ((before_ref, early_ks), (x_ref, late_ks)):
        x = (scale * ref[...].astype(jnp.float32)).astype(jnp.bfloat16)
        new = ((3.4445 - shift) * x.astype(jnp.float32) + mm(w_ref[...], x)).astype(jnp.bfloat16)
        for i, k in enumerate(ks):
            y_ref[:, k * cols : (k + 1) * cols] = new[:, i * cols : (i + 1) * cols]
    symmetric(y_ref, h_ref)
    for k in sorted({k for pieces in plan for k, _ in pieces}):
        new = step_columns(h_ref, y_ref[:, k * cols : (k + 1) * cols], power_ref)
        finish(new.astype(jnp.bfloat16), k, plan, outs)


def first(early_ks, before, part, sums, late, plan, after):
    shards, rows, cols = late[max(late)].shape
    order = shards * rows
    late_ks = sorted(late)
    square = jax.ShapeDtypeStruct((order, order), jnp.bfloat16)
    return pl.pallas_call(
        functools.partial(first_kernel, early_ks, late_ks, plan),
        in_specs=[whole()] * (3 + len(late)) + [whole(pl.ANY)],
        out_specs=[whole()] * (2 + len(plan)),
        out_shape=[square, square]
        + [jax.ShapeDtypeStruct((len(pieces), rows, cols), jnp.bfloat16) for pieces in plan],
        scratch_shapes=[pltpu.VMEM((order, len(late) * cols), jnp.bfloat16)]
        + [pltpu.VMEM((order, order), jnp.bfloat16)] * 2
        + [pltpu.VMEM((order, cols), jnp.float32)],
        compiler_params=params(20),
        cost_estimate=cost(7 * order**3, 12 * order**2),
    )(before, part, sums, *[late[k] for k in late_ks], after)


def last_kernel(plan, x_ref, g_ref, *refs):
    outs, power_ref = refs[:-1], refs[-1]
    order = x_ref.shape[0]
    ks = sorted({k for pieces in plan for k, _ in pieces}, reverse=True)
    cols = power_ref.shape[1] // len(ks)
    x = jnp.concatenate([x_ref[:, k * cols : (k + 1) * cols] for k in ks], axis=1)
    new = step_columns(g_ref, x, power_ref).astype(jnp.bfloat16)
    for i, k in enumerate(ks):
        finish(new[:, i * cols : (i + 1) * cols], k, plan, outs)


def last(x, g, plan, rows, cols):
    order = x.shape[0]
    return pl.pallas_call(
        functools.partial(last_kernel, plan),
        in_specs=[whole()] * 2,
        out_specs=[whole()] * len(plan),
        out_shape=[jax.ShapeDtypeStruct((len(pieces), rows, cols), jnp.bfloat16) for pieces in plan],
        scratch_shapes=[pltpu.VMEM((order, len({k for p in plan for k, _ in p}) * cols), jnp.float32)],
        compiler_params=params(16),
        cost_estimate=cost(len(plan) // 8 * order**3 + order**3, 8 * order**2),
    )(x, g)


def place_kernel(places, shards, *refs):
    o_ref, sems = refs[-2:]
    t, s = lax.axis_index("tensor"), lax.axis_index("shard")
    copies = []
    for n, (k, u, which, b) in enumerate(places):
        group = (t ^ k) * shards
        if b is None:
            src, dst = refs[which], o_ref.at[pl.ds(group, shards)]
        else:
            src, dst = refs[which].at[b], o_ref.at[group + (s ^ u)]
        copies.append(pltpu.make_async_copy(src, dst, sems.at[n]))
    for c in copies:
        c.start()
    for c in copies:
        c.wait()


def place(chunks, shards, shape, before):
    arrays, places = arrays_of(chunks)
    more = [] if before is None else [before]
    return pl.pallas_call(
        functools.partial(place_kernel, places, shards),
        in_specs=[whole()] * len(arrays) + [whole(pltpu.HBM)] * len(more),
        out_specs=whole(pltpu.HBM),
        out_shape=jax.ShapeDtypeStruct(shape, jnp.bfloat16),
        scratch_shapes=[pltpu.SemaphoreType.DMA((len(places),))],
        input_output_aliases={len(arrays): 0} if more else {},
        compiler_params=params(8),
        cost_estimate=cost(1000, 1000),
    )(*arrays, *more)


def shards(grads, momentum):
    count, rows, cols = grads.shape
    shard_count = lax.axis_size("shard")
    t = lax.axis_index("tensor")
    ks = early_k, late_k = FWD
    _, p31_plan, a0_plan = plans(shard_count, *ks)
    z2 = nesterov_group(grads, momentum, t ^ early_k, shard_count)
    z2, grads, momentum = lax.optimization_barrier((z2, grads, momentum))
    p31 = nesterov(grads, momentum, p31_plan, shard_count)
    (a0,) = nesterov(grads, momentum, a0_plan, shard_count)
    chunks = exchange(z2, p31, a0, True, *ks)
    momentum_next, token = next_momentum(grads, momentum, chunks[0][0][0])
    before, part, sums = early({k: chunks[k] for k in (0, early_k)})
    late = {k: chunks[k][0][0] for k in (1, late_k)}
    fk = early_k

    ks = early_k, late_k = BACK
    z2_plan, p31_plan, a0_plan = plans(shard_count, *ks)
    x, g, z2 = first((0, fk), before, part, sums, late, z2_plan, token)
    p31 = list(last(x, g, p31_plan, rows, cols))
    (a0,) = last(x, g, a0_plan, rows, cols)
    back = exchange(z2, p31, a0, False, *ks)
    update = place({k: back[k] for k in (0, early_k)}, shard_count, grads.shape, None)
    update = place({k: back[k] for k in (1, late_k)}, shard_count, grads.shape, update)
    return (momentum_next, update)


def solution(mesh):
    return jax.shard_map(
        shards,
        mesh=mesh,
        in_specs=(P(None, "shard", "tensor"), P(None, "shard", "tensor")),
        out_specs=(P(None, "shard", "tensor"), P(None, "shard", "tensor")),
        check_vma=False,
    )
```
